512 devices in a mesh: rep: 8 (over y_hi, core), dap: 64 (over z, y_lo, x).
Axes of the slice: x: 4, y: 8 (y_hi: 4, y_lo: 2; y = y_hi * 2 + y_lo), z: 8, core: 2. Of those that a mesh axis runs over, the one named last changes fastest.
Arguments:
- pair_act: bfloat16 [8, 256, 256, 128], P('rep', 'dap'), may hold values from -6 to 6
- cotangent: bfloat16 [8, 256, 256, 128], P('rep', 'dap'), may hold values from -6 to 6
- outgoing_in: bfloat16 [128, 640], replicated, may hold values from -0.5 to 0.5
- outgoing_out: bfloat16 [128, 128], replicated, may hold values from -0.5 to 0.5
- incoming_in: bfloat16 [128, 640], replicated, may hold values from -0.5 to 0.5
- incoming_out: bfloat16 [128, 128], replicated, may hold values from -0.5 to 0.5
Outputs:
- pair_grad: bfloat16 [8, 256, 256, 128], P('rep', 'dap')
- outgoing_in_grad: float32 [128, 640], replicated
- outgoing_out_grad: float32 [128, 128], replicated
- incoming_in_grad: float32 [128, 640], replicated
- incoming_out_grad: float32 [128, 128], replicated
The draws below stay inside these ranges and needn't reach their ends.
All inputs are finite; a program needn't handle non-finite values.
Results may differ from the reference program's by a relative error of at most 0.019.
Values may be sent and summed in bfloat16 or wider, within the bound.
No kernel may reach another device: no remote copies, remote signals or barrier semaphores. Data moves between devices by JAX's collectives and lax.ppermute only.
A program may use at most 64 MiB of HBM per device.

```python
import math
import jax
import jax.numpy as jnp
from jax import lax

CZ = 128
CH = 128
N = 256
CROPS = 8


def shard_levels(own_key, dims, split, low, high):
    def one(dim, blocks):
        steps = jax.random.uniform(jax.random.fold_in(jax.random.fold_in(own_key, 6), dim), (blocks,), jnp.float32, low / len(split), high / len(split))
        return jnp.repeat(jnp.exp(steps), dims[dim] // blocks).reshape((-1,) + (1,) * (len(dims) - dim - 1))

    level = one(*split[0])
    for cut in split[1:]:
        level = level * one(*cut)
    return level


def gaussian(rng, shape, scale, reach, shards=(), dtype=jnp.bfloat16):
    drawn = scale * jax.random.normal(rng, shape, jnp.float32)
    if shards:
        drawn = drawn * shard_levels(rng, shape, shards, -0.22, 0.18)
    return jnp.clip(drawn, -reach, reach).astype(dtype)


def setup_inputs(seed: int = 0) -> dict:
    arg_keys = jax.random.split(jax.random.key(seed), 7)
    return {
        "pair_act": gaussian(arg_keys[0], (CROPS, N, N, CZ), 1.0, 6.0, ((0, 8), (1, 64))),
        "cotangent": gaussian(arg_keys[1], (CROPS, N, N, CZ), 1.0, 6.0, ((0, 8), (1, 64))),
        "outgoing_in": gaussian(arg_keys[2], (CZ, 4 * CH + CZ), CZ ** -0.5, 0.5),
        "outgoing_out": gaussian(arg_keys[3], (CH, CZ), CH ** -0.5, 0.5),
        "incoming_in": gaussian(arg_keys[4], (CZ, 4 * CH + CZ), CZ ** -0.5, 0.5),
        "incoming_out": gaussian(arg_keys[5], (CH, CZ), CH ** -0.5, 0.5),
    }


EPS = 1e-05

def normalize(values, along):
    average = lax.optimization_barrier(jnp.mean(values, axis=along, keepdims=True))
    centred = values - average
    spread = lax.optimization_barrier(jnp.mean(centred * centred, axis=along, keepdims=True))
    inv_std = lax.rsqrt(spread + EPS)
    return (centred * inv_std, inv_std)

def norm_back(normed, inv_std, incoming_grad, along):
    first = lax.optimization_barrier(jnp.mean(incoming_grad, axis=along, keepdims=True))
    second = lax.optimization_barrier(jnp.mean(incoming_grad * normed, axis=along, keepdims=True))
    return inv_std * (incoming_grad - first - normed * second)

def module_forward(state, w_in, w_out, incoming):
    length = state.shape[0]
    width = state.shape[2]
    hidden = w_out.shape[0]
    normed, inv_std = normalize(state, 2)
    normed_in = normed.astype(jnp.bfloat16)
    projected = jnp.dot(normed_in.reshape(-1, width), w_in, preferred_element_type=jnp.float32).reshape(length, length, -1)
    left_proj = projected[:, :, :hidden]
    left_gate = projected[:, :, hidden:2 * hidden]
    right_proj = projected[:, :, 2 * hidden:3 * hidden]
    right_gate = projected[:, :, 3 * hidden:4 * hidden]
    gate_logits = projected[:, :, 4 * hidden:]
    left_op = (jax.nn.sigmoid(left_gate) * left_proj).astype(jnp.bfloat16)
    right_op = (jax.nn.sigmoid(right_gate) * right_proj).astype(jnp.bfloat16)
    if incoming:
        product = jnp.einsum('kic,kjc->ijc', left_op.astype(jnp.float32), right_op.astype(jnp.float32))
    else:
        product = jnp.einsum('ikc,jkc->ijc', left_op.astype(jnp.float32), right_op.astype(jnp.float32))
    product = product.astype(jnp.bfloat16)
    out_normed, out_inv = normalize(product.astype(jnp.float32), 2)
    out_bf = out_normed.astype(jnp.bfloat16)
    mixed = jnp.dot(out_bf.reshape(-1, hidden), w_out, preferred_element_type=jnp.float32).reshape(length, length, width)
    gate_val = jax.nn.sigmoid(gate_logits)
    saved = (normed, inv_std, normed_in, left_proj, left_gate, right_proj, right_gate, left_op, right_op, out_normed, out_inv, out_bf, mixed, gate_val)
    return (state + gate_val * mixed, saved)

def module_backward(grad_u, saved, w_in, w_out, incoming):
    normed, inv_std, normed_in, left_proj, left_gate, right_proj, right_gate, left_op, right_op, out_normed, out_inv, out_bf, mixed, gate_val = saved
    length = grad_u.shape[0]
    width = grad_u.shape[2]
    hidden = w_out.shape[0]
    grad_mix = (grad_u * gate_val).astype(jnp.bfloat16)
    grad_gate = grad_u * mixed * gate_val * (1.0 - gate_val)
    grad_out_w = jnp.dot(out_bf.reshape(-1, hidden).T, grad_mix.reshape(-1, width), preferred_element_type=jnp.float32)
    grad_on = jnp.dot(grad_mix.reshape(-1, width), w_out.T, preferred_element_type=jnp.float32).reshape(length, length, hidden)
    grad_prod = norm_back(out_normed, out_inv, grad_on, 2).astype(jnp.bfloat16).astype(jnp.float32)
    left_f = left_op.astype(jnp.float32)
    right_f = right_op.astype(jnp.float32)
    if incoming:
        grad_left = jnp.einsum('ijc,kjc->kic', grad_prod, right_f)
        grad_right = jnp.einsum('ijc,kic->kjc', grad_prod, left_f)
    else:
        grad_left = jnp.einsum('ijc,jkc->ikc', grad_prod, right_f)
        grad_right = jnp.einsum('ijc,ikc->jkc', grad_prod, left_f)
    grad_left = grad_left.astype(jnp.bfloat16)
    grad_right = grad_right.astype(jnp.bfloat16)
    sig_left = jax.nn.sigmoid(left_gate)
    sig_right = jax.nn.sigmoid(right_gate)
    grad_pre = jnp.concatenate([grad_left * sig_left, grad_left * left_proj * sig_left * (1.0 - sig_left), grad_right * sig_right, grad_right * right_proj * sig_right * (1.0 - sig_right), grad_gate], 2).astype(jnp.bfloat16)
    grad_in_w = jnp.dot(normed_in.reshape(-1, width).T, grad_pre.reshape(-1, 4 * hidden + width), preferred_element_type=jnp.float32)
    grad_normed = jnp.dot(grad_pre.reshape(-1, 4 * hidden + width), w_in.T, preferred_element_type=jnp.float32).reshape(length, length, width)
    return (grad_u + norm_back(normed, inv_std, grad_normed, 2), grad_in_w, grad_out_w)

def reference(pair_act, cotangent, outgoing_in, outgoing_out, incoming_in, incoming_out):
    pair_rows = []
    total_oi = jnp.zeros(outgoing_in.shape, jnp.float32)
    total_oo = jnp.zeros(outgoing_out.shape, jnp.float32)
    total_ii = jnp.zeros(incoming_in.shape, jnp.float32)
    total_io = jnp.zeros(incoming_out.shape, jnp.float32)
    for crop in range(CROPS):
        start = pair_act[crop].astype(jnp.float32)
        middle, saved_out = module_forward(start, outgoing_in, outgoing_out, False)
        finish, saved_in = module_forward(middle, incoming_in, incoming_out, True)
        grad_mid, grad_ii, grad_io = module_backward(cotangent[crop].astype(jnp.float32), saved_in, incoming_in, incoming_out, True)
        grad_start, grad_oi, grad_oo = module_backward(grad_mid, saved_out, outgoing_in, outgoing_out, False)
        pair_rows.append(grad_start.astype(jnp.bfloat16))
        total_oi = total_oi + grad_oi
        total_oo = total_oo + grad_oo
        total_ii = total_ii + grad_ii
        total_io = total_io + grad_io
    grad_scale = 1.0 / math.sqrt(CROPS * N * N)
    return (jnp.stack(pair_rows, 0), total_oi * grad_scale, total_oo * grad_scale, total_ii * grad_scale, total_io * grad_scale)
```

```python
import math

import jax
import jax.numpy as jnp
from jax import lax
from jax.experimental import pallas as pl
from jax.experimental.pallas import tpu as pltpu
from jax.sharding import PartitionSpec as P

EPS = 1e-05
ROWS = 4
N = 256
C = 128
BF = jnp.bfloat16
F32 = jnp.float32
VMEM_LIMIT = 48 * 1024 * 1024


def dot(a, b, ca, cb):
    return lax.dot_general(a, b, (((ca,), (cb,)), ((), ())), preferred_element_type=F32)


def swap():
    row = lax.broadcasted_iota(jnp.int32, (256, 256), 0)
    col = lax.broadcasted_iota(jnp.int32, (256, 256), 1)
    hit = ((row & 15) == (col >> 4)) & ((row >> 4) == (col & 15))
    return jnp.where(hit, 1.0, 0.0).astype(BF)


def column_order():
    row = lax.broadcasted_iota(jnp.int32, (N, N), 0)
    col = lax.broadcasted_iota(jnp.int32, (N, N), 1)
    return jnp.where(col == 4 * (row & 63) + (row >> 6), 1.0, 0.0).astype(BF)


def norm(x):
    centred = x - jnp.mean(x, axis=0, keepdims=True)
    inv = lax.rsqrt(jnp.mean(centred * centred, axis=0, keepdims=True) + EPS)
    return centred * inv, inv


def norm_back(normed, inv, grad):
    first = jnp.mean(grad, axis=0, keepdims=True)
    second = jnp.mean(grad * normed, axis=0, keepdims=True)
    return inv * (grad - first - normed * second)


def pack(msg, piece):
    s = swap()
    for big in range(4):
        x = jnp.concatenate([piece(q, big) for q in range(16)], axis=0)
        msg[pl.ds(256 * big, 256), :] = dot(s, x, 1, 0).astype(BF)


def unpack(msg, put):
    s = swap()
    for big in range(4):
        y = dot(s, msg[pl.ds(256 * big, 256), :], 1, 0).astype(BF)
        for q in range(16):
            put(q, big, y[16 * q : 16 * q + 16, :])


def pack_pair(msg, cells):
    def piece(q, big):
        t, m, r = q // 8, (q // 4) % 2, q % 4
        return cells[pl.ds((t * ROWS + r) * C + m * 64 + 16 * big, 16), :]

    pack(msg, piece)


def unpack_pair(msg, cells):
    def put(q, big, rows):
        t, m, r = q // 8, (q // 4) % 2, q % 4
        cells[pl.ds((t * ROWS + r) * C + m * 64 + 16 * big, 16), :] = rows

    unpack(msg, put)


def pack_one(msg, cells):
    def piece(q, big):
        h, m, r = q // 8, (q // 4) % 2, q % 4
        return cells[pl.ds(r * C + m * 64 + 16 * big, 16), pl.ds(128 * h, 128)]

    pack(msg, piece)


def unpack_one(msg, cells):
    def put(q, big, rows):
        h, m, r = q // 8, (q // 4) % 2, q % 4
        cells[pl.ds(r * C + m * 64 + 16 * big, 16), pl.ds(128 * h, 128)] = rows

    unpack(msg, put)


def row(ref, r):
    return ref[pl.ds(r * C, C), :]


def gated(nb, w):
    pre = dot(w[:, : 4 * C], nb, 0, 0)
    return pre[:C], jax.nn.sigmoid(pre[C : 2 * C]), pre[2 * C : 3 * C], jax.nn.sigmoid(pre[3 * C :])


def gate_of(nb, w):
    return jax.nn.sigmoid(dot(w[:, 4 * C :], nb, 0, 0))


def operands(state, w, r, cells):
    normed, _ = norm(state)
    left, left_s, right, right_s = gated(normed.astype(BF), w)
    cells[pl.ds(r * C, C), :] = (left_s * left).astype(BF)
    cells[pl.ds((ROWS + r) * C, C), :] = (right_s * right).astype(BF)


def first_kernel(u, w1, msg, u_t, cells):
    order = column_order()
    w = w1[...]
    for r in range(ROWS):
        state = dot(u[r], order, 0, 1)
        u_t[pl.ds(r * C, C), :] = state.astype(BF)
        operands(state, w, r, cells)
    pack_pair(msg, cells)


def product_kernel(incoming, msg, kept, out, prod):
    def put(q, big, rows):
        t, m, r = q // 8, (q // 4) % 2, q % 4
        kept[pl.ds((2 * t + m) * N + 64 * r + 16 * big, 16), :] = rows

    unpack(msg, put)
    over = 0 if incoming else 1
    for m in range(2):
        left = kept[pl.ds(m * N, N), :]
        right = kept[pl.ds((2 + m) * N, N), :]
        prod[pl.ds(m * N, N), :] = dot(left, right, over, over).astype(BF)

    def piece(q, big):
        h, m, r = q // 8, (q // 4) % 2, q % 4
        return prod[pl.ds(m * N + 64 * r + 16 * big, 16), pl.ds(128 * h, 128)]

    pack(out, piece)


def middle_kernel(pmsg, u_t, w1, v1, w2, msg, z1, prod, cells):
    unpack_one(pmsg, prod)
    w, v, w_next = w1[...], v1[...], w2[...]
    for r in range(ROWS):
        state = row(u_t, r).astype(F32)
        gate = gate_of(norm(state)[0].astype(BF), w)
        out_bf = norm(row(prod, r).astype(F32))[0].astype(BF)
        state = state + gate * dot(v, out_bf, 0, 0)
        z1[pl.ds(r * C, C), :] = state
        operands(state, w_next, r, cells)
    pack_pair(msg, cells)


def cotangent_kernel(cot, z1, w2, v2, cot_t, mix, grad_on):
    order = column_order()
    w, v = w2[...], v2[...]
    for r in range(ROWS):
        grad_u = dot(cot[r], order, 0, 1)
        cot_t[pl.ds(r * C, C), :] = grad_u.astype(BF)
        gate = gate_of(norm(row(z1, r))[0].astype(BF), w)
        grad_mix = (grad_u * gate).astype(BF)
        mix[pl.ds(r * C, C), :] = grad_mix
        grad_on[pl.ds(r * C, C), :] = dot(v, grad_mix, 1, 0)


def turn_kernel(pmsg, grad_on, msg, prod, cells):
    unpack_one(pmsg, prod)
    for r in range(ROWS):
        normed, inv = norm(row(prod, r).astype(F32))
        cells[pl.ds(r * C, C), :] = norm_back(normed, inv, row(grad_on, r)).astype(BF)
    pack_one(msg, cells)


def gate_grads(grad_u, mix, prod, state, w, v):
    nb = norm(state)[0].astype(BF)
    gate = gate_of(nb, w)
    out_bf = norm(prod.astype(F32))[0].astype(BF)
    mixed = dot(v, out_bf, 0, 0)
    grad_gate = (grad_u * mixed * gate * (1.0 - gate)).astype(BF)
    return grad_gate, dot(out_bf, mix, 1, 1), dot(nb, grad_gate, 1, 1)


def late_kernel(grad_u, mix, prod, state, w_ref, v_ref, grad_gate, sums):
    w, v = w_ref[...], v_ref[...]
    grad_v = grad_w = 0.0
    for r in range(ROWS):
        gg, gv, gw = gate_grads(
            row(grad_u, r).astype(F32), row(mix, r), row(prod, r), row(state, r).astype(F32), w, v
        )
        grad_gate[pl.ds(r * C, C), :] = gg
        grad_v = grad_v + gv
        grad_w = grad_w + gw
    sums[pl.ds(0, C), :] = grad_w.astype(BF)
    sums[pl.ds(C, C), :] = grad_v.astype(BF)


def grads_kernel(incoming, gmsg, kept, msg, prod, sides):
    def put(q, big, rows):
        h, m, r = q // 8, (q // 4) % 2, q % 4
        prod[pl.ds(m * N + 64 * r + 16 * big, 16), pl.ds(128 * h, 128)] = rows

    unpack(gmsg, put)
    for m in range(2):
        left = kept[pl.ds(m * N, N), :]
        right = kept[pl.ds((2 + m) * N, N), :]
        grad = prod[pl.ds(m * N, N), :]
        if incoming:
            grad_left, grad_right = dot(right, grad, 1, 1), dot(left, grad, 1, 0)
        else:
            grad_left, grad_right = dot(grad, right, 1, 0), dot(grad, left, 0, 0)
        sides[pl.ds(m * N, N), :] = grad_left.astype(BF)
        sides[pl.ds((2 + m) * N, N), :] = grad_right.astype(BF)

    def piece(q, big):
        t, m, r = q // 8, (q // 4) % 2, q % 4
        return sides[pl.ds((2 * t + m) * N + 64 * r + 16 * big, 16), :]

    pack(msg, piece)


def project_grad(cells, r, nb, w):
    left, left_s, right, right_s = gated(nb, w)
    grad_left = cells[pl.ds(r * C, C), :].astype(F32) * left_s
    grad_right = cells[pl.ds((ROWS + r) * C, C), :].astype(F32) * right_s
    return jnp.concatenate(
        [
            grad_left.astype(BF),
            (grad_left * left * (1.0 - left_s)).astype(BF),
            grad_right.astype(BF),
            (grad_right * right * (1.0 - right_s)).astype(BF),
        ],
        0,
    )


def input_grad(grad_u, normed, inv, grad_proj, grad_gate, w):
    grad = dot(w[:, : 4 * C], grad_proj, 1, 0) + dot(w[:, 4 * C :], grad_gate, 1, 0)
    return grad_u + norm_back(normed, inv, grad)


def back_kernel(
    gmsg, z1, gg2, cot_t, w2, u_t, prod1, w1, v1, msg, proj, grad_u, mix, cells, grad_prod
):
    unpack_pair(gmsg, cells)
    w_in, w, v = w2[...], w1[...], v1[...]
    for r in range(ROWS):
        normed, inv = norm(row(z1, r))
        grad_proj = project_grad(cells, r, normed.astype(BF), w_in)
        proj[pl.ds(4 * r * C, 4 * C), :] = grad_proj
        grad = input_grad(row(cot_t, r).astype(F32), normed, inv, grad_proj, row(gg2, r), w_in)
        grad_u[pl.ds(r * C, C), :] = grad
        gate = gate_of(norm(row(u_t, r).astype(F32))[0].astype(BF), w)
        grad_mix = (grad * gate).astype(BF)
        mix[pl.ds(r * C, C), :] = grad_mix
        normed, inv = norm(row(prod1, r).astype(F32))
        grad_prod[pl.ds(r * C, C), :] = norm_back(normed, inv, dot(v, grad_mix, 1, 0)).astype(BF)
    pack_one(msg, grad_prod)


def weight_kernel(state, proj, sums):
    total = 0.0
    for r in range(ROWS):
        nb = norm(row(state, r).astype(F32))[0].astype(BF)
        total = total + dot(proj[pl.ds(4 * r * C, 4 * C), :], nb, 1, 1)
    sums[...] = total.astype(BF)


def last_kernel(gmsg, u_t, w1, lr2, gv2, gv1, msg, proj, cells):
    unpack_pair(gmsg, cells)
    w = w1[...]
    total = 0.0
    for r in range(ROWS):
        nb = norm(row(u_t, r).astype(F32))[0].astype(BF)
        grad_proj = project_grad(cells, r, nb, w)
        proj[pl.ds(4 * r * C, 4 * C), :] = grad_proj
        total = total + dot(grad_proj, nb, 1, 1)
    msg[pl.ds(0, 4 * C), :] = total.astype(BF)
    msg[pl.ds(4 * C, 2 * C), :] = gv1[...]
    msg[pl.ds(6 * C, 4 * C), :] = lr2[...]
    msg[pl.ds(10 * C, 2 * C), :] = gv2[...]


def pair_kernel(u_t, proj, gg1, grad_u, w1, out):
    order = column_order()
    w = w1[...]
    for r in range(ROWS):
        normed, inv = norm(row(u_t, r).astype(F32))
        grad = input_grad(
            row(grad_u, r), normed, inv, proj[pl.ds(4 * r * C, 4 * C), :], row(gg1, r), w
        )
        out[r] = dot(order, grad.astype(BF), 0, 1).astype(BF)


def finish_kernel(sums, oi, oo, ii, io):
    for base, w, v in ((0, oi, oo), (6 * C, ii, io)):
        for b in range(4):
            w[:, pl.ds(b * C, C)] = sums[pl.ds(base + b * C, C), :].astype(F32).T
        w[:, pl.ds(4 * C, C)] = sums[pl.ds(base + 4 * C, C), :].astype(F32)
        v[...] = sums[pl.ds(base + 5 * C, C), :].astype(F32)


def call(kernel, outs, scratch, *args, name, flops=2e8):
    shapes = [jax.ShapeDtypeStruct(s, d) for s, d in outs]
    moved = sum(a.size * a.dtype.itemsize for a in args)
    moved += sum(s.size * s.dtype.itemsize for s in shapes)
    return pl.pallas_call(
        kernel,
        out_shape=shapes,
        scratch_shapes=[pltpu.VMEM(s, d) for s, d in scratch],
        compiler_params=pltpu.CompilerParams(vmem_limit_bytes=VMEM_LIMIT),
        cost_estimate=pl.CostEstimate(
            flops=int(flops), bytes_accessed=int(moved), transcendentals=0
        ),
        name=name,
    )(*args)


def exchange(msg):
    shape = msg.shape
    out = lax.all_to_all(msg.reshape(64, 16, shape[1]), "dap", 0, 0, tiled=True)
    return out.reshape(shape)


ONE = (ROWS * C, N)
TWO = (2 * ROWS * C, N)
ONE_MSG = (64 * 16, 128)
TWO_MSG = (64 * 16, 256)
PROJ = (4 * ROWS * C, N)


def product(msg, incoming):
    def kernel(*refs):
        product_kernel(incoming, *refs)

    return call(
        kernel, [((4 * N, N), BF), (ONE_MSG, BF)], [((2 * N, N), BF)], msg, name="product"
    )


def grads(gmsg, kept, incoming):
    def kernel(*refs):
        grads_kernel(incoming, *refs)

    return call(
        kernel, [(TWO_MSG, BF)], [((2 * N, N), BF), ((4 * N, N), BF)], gmsg, kept, name="grads"
    )[0]


def local(pair_act, cotangent, w1, v1, w2, v2):
    lr1, u_t = call(
        first_kernel, [(TWO_MSG, BF), (ONE, BF)], [(TWO, BF)], pair_act[0], w1, name="first"
    )
    kept1, pmsg1 = product(exchange(lr1), False)
    lr2, z1, prod1 = call(
        middle_kernel,
        [(TWO_MSG, BF), (ONE, F32), (ONE, BF)],
        [(TWO, BF)],
        exchange(pmsg1), u_t, w1, v1, w2,
        name="middle",
    )
    cot_t, mix2, grad_on2 = call(
        cotangent_kernel,
        [(ONE, BF), (ONE, BF), (ONE, F32)],
        [],
        cotangent[0], z1, w2, v2,
        name="cotangent",
    )
    kept2, pmsg2 = product(exchange(lr2), True)
    gmsg2, prod2 = call(
        turn_kernel, [(ONE_MSG, BF), (ONE, BF)], [(ONE, BF)], exchange(pmsg2), grad_on2, name="turn"
    )
    gg2, gv2 = call(
        late_kernel,
        [(ONE, BF), ((2 * C, C), BF)],
        [],
        cot_t, mix2, prod2, z1, w2, v2,
        name="late_incoming",
    )
    gsides2 = grads(exchange(gmsg2), kept2, True)
    gmsg1, proj2, grad_u1, mix1 = call(
        back_kernel,
        [(ONE_MSG, BF), (PROJ, BF), (ONE, F32), (ONE, BF)],
        [(TWO, BF), (ONE, BF)],
        exchange(gsides2), z1, gg2, cot_t, w2, u_t, prod1, w1, v1,
        name="back",
    )
    sums2 = call(weight_kernel, [((4 * C, C), BF)], [], z1, proj2, name="weights_incoming")[0]
    gg1, gv1 = call(
        late_kernel,
        [(ONE, BF), ((2 * C, C), BF)],
        [],
        grad_u1, mix1, prod1, u_t, w1, v1,
        name="late_outgoing",
    )
    gsides1 = grads(exchange(gmsg1), kept1, False)
    wmsg, proj1 = call(
        last_kernel,
        [((12 * C, C), BF), (PROJ, BF)],
        [(TWO, BF)],
        exchange(gsides1), u_t, w1, sums2, gv2, gv1,
        name="last",
    )
    pair_grad = call(
        pair_kernel, [((ROWS, N, C), BF)], [], u_t, proj1, gg1, grad_u1, w1, name="pair"
    )[0]

    scale = 1.0 / math.sqrt(lax.axis_size("rep") * pair_act.shape[0] * N * N)
    parts = lax.all_to_all(wmsg.reshape(64, 24, C), "dap", 0, 0, tiled=True)
    part = jnp.sum(parts.astype(F32), axis=0)
    reps = lax.axis_size("rep")
    across = lax.all_to_all(jnp.broadcast_to(part, (reps, 24, C)), "rep", 0, 0, tiled=True)
    whole = (jnp.sum(across, axis=0) * scale).astype(BF)
    everywhere = lax.all_to_all(jnp.broadcast_to(whole, (64, 24, C)), "dap", 0, 0, tiled=True)
    oi, oo, ii, io = call(
        finish_kernel,
        [((C, 5 * C), F32), ((C, C), F32), ((C, 5 * C), F32), ((C, C), F32)],
        [],
        everywhere.reshape(12 * C, C),
        name="finish",
    )
    return pair_grad[None], oi, oo, ii, io


def solution(mesh):
    return jax.shard_map(
        local,
        mesh=mesh,
        in_specs=(P("rep", "dap", None, None), P("rep", "dap", None, None), P(), P(), P(), P()),
        out_specs=(P("rep", "dap", None, None), P(), P(), P(), P()),
        check_vma=False,
    )
```

```python
import math

import jax
import jax.numpy as jnp
from jax import lax
from jax.experimental import pallas as pl
from jax.experimental.pallas import tpu as pltpu
from jax.sharding import PartitionSpec as P

EPS = 1e-05
ROWS = 4
N = 256
C = 128
BF = jnp.bfloat16
F32 = jnp.float32
VMEM_LIMIT = 48 * 1024 * 1024


def dot(a, b, ca, cb):
    return lax.dot_general(a, b, (((ca,), (cb,)), ((), ())), preferred_element_type=F32)


def swap():
    row = lax.broadcasted_iota(jnp.int32, (256, 256), 0)
    col = lax.broadcasted_iota(jnp.int32, (256, 256), 1)
    hit = ((row & 15) == (col >> 4)) & ((row >> 4) == (col & 15))
    return jnp.where(hit, 1.0, 0.0).astype(BF)


def column_order():
    row = lax.broadcasted_iota(jnp.int32, (N, N), 0)
    col = lax.broadcasted_iota(jnp.int32, (N, N), 1)
    return jnp.where(col == 4 * (row & 63) + (row >> 6), 1.0, 0.0).astype(BF)


def norm(x):
    centred = x - jnp.mean(x, axis=0, keepdims=True)
    inv = lax.rsqrt(jnp.mean(centred * centred, axis=0, keepdims=True) + EPS)
    return centred * inv, inv


def norm_back(normed, inv, grad):
    first = jnp.mean(grad, axis=0, keepdims=True)
    second = jnp.mean(grad * normed, axis=0, keepdims=True)
    return inv * (grad - first - normed * second)


def pack(msg, piece):
    s = swap()
    for big in range(4):
        x = jnp.concatenate([piece(q, big) for q in range(16)], axis=0)
        msg[pl.ds(256 * big, 256), :] = dot(s, x, 1, 0).astype(BF)


def unpack(msg, put):
    s = swap()
    for big in range(4):
        y = dot(s, msg[pl.ds(256 * big, 256), :], 1, 0).astype(BF)
        for q in range(16):
            put(q, big, y[16 * q : 16 * q + 16, :])


def pack_pair(msg, cells):
    def piece(q, big):
        t, m, r = q // 8, (q // 4) % 2, q % 4
        return cells[pl.ds((t * ROWS + r) * C + m * 64 + 16 * big, 16), :]

    pack(msg, piece)


def unpack_pair(msg, cells):
    def put(q, big, rows):
        t, m, r = q // 8, (q // 4) % 2, q % 4
        cells[pl.ds((t * ROWS + r) * C + m * 64 + 16 * big, 16), :] = rows

    unpack(msg, put)


def pack_one(msg, cells):
    def piece(q, big):
        h, m, r = q // 8, (q // 4) % 2, q % 4
        return cells[pl.ds(r * C + m * 64 + 16 * big, 16), pl.ds(128 * h, 128)]

    pack(msg, piece)


def unpack_one(msg, cells):
    def put(q, big, rows):
        h, m, r = q // 8, (q // 4) % 2, q % 4
        cells[pl.ds(r * C + m * 64 + 16 * big, 16), pl.ds(128 * h, 128)] = rows

    unpack(msg, put)


def row(ref, r):
    return ref[pl.ds(r * C, C), :]


def gated(nb, w):
    pre = dot(w[:, : 4 * C], nb, 0, 0)
    return pre[:C], jax.nn.sigmoid(pre[C : 2 * C]), pre[2 * C : 3 * C], jax.nn.sigmoid(pre[3 * C :])


def gate_of(nb, w):
    return jax.nn.sigmoid(dot(w[:, 4 * C :], nb, 0, 0))


def operands(state, w, r, cells):
    normed, _ = norm(state)
    left, left_s, right, right_s = gated(normed.astype(BF), w)
    cells[pl.ds(r * C, C), :] = (left_s * left).astype(BF)
    cells[pl.ds((ROWS + r) * C, C), :] = (right_s * right).astype(BF)


def prepare(state, cot, w, order, r, cot_t, gate, nb, factors):
    cot_t[pl.ds(r * C, C), :] = dot(cot[r], order, 0, 1).astype(BF)
    normed_in = norm(state)[0].astype(BF)
    nb[pl.ds(r * C, C), :] = normed_in
    gate[pl.ds(r * C, C), :] = gate_of(normed_in, w)
    store_factors(factors, r, gated(normed_in, w))


def store_factors(factors, r, sides):
    left, left_s, right, right_s = sides
    for b, x in enumerate(
        (left_s, left * left_s * (1.0 - left_s), right_s, right * right_s * (1.0 - right_s))
    ):
        factors[pl.ds((4 * r + b) * C, C), :] = x.astype(BF)


def first_kernel(core, u, cot, w1, msg, u_t, cot_t, gate, nb, factors, cells):
    order = column_order()
    w = w1[...]
    for r in range(ROWS):
        state = dot(u[r], order, 0, 1)
        u_t[pl.ds(r * C, C), :] = state.astype(BF)
        operands(state, w, r, cells)
    pack_pair(msg, cells)

    @pl.when(core[0] == 0)
    def _():
        for r in range(ROWS):
            prepare(row(u_t, r).astype(F32), cot, w, order, r, cot_t, gate, nb, factors)


def second_kernel(core, u_t, cot, w1, *refs):
    made, kept = refs[:4], refs[4:]

    @pl.when(core[0] == 0)
    def _():
        for old, new in zip(made, kept):
            new[...] = old[...]

    @pl.when(core[0] != 0)
    def _():
        order = column_order()
        w = w1[...]
        for r in range(ROWS):
            prepare(row(u_t, r).astype(F32), cot, w, order, r, *kept)


def product_kernel(incoming, msg, kept, out, prod):
    def put(q, big, rows):
        t, m, r = q // 8, (q // 4) % 2, q % 4
        kept[pl.ds((2 * t + m) * N + 64 * r + 16 * big, 16), :] = rows

    unpack(msg, put)
    over = 0 if incoming else 1
    for m in range(2):
        left = kept[pl.ds(m * N, N), :]
        right = kept[pl.ds((2 + m) * N, N), :]
        prod[pl.ds(m * N, N), :] = dot(left, right, over, over).astype(BF)

    def piece(q, big):
        h, m, r = q // 8, (q // 4) % 2, q % 4
        return prod[pl.ds(m * N + 64 * r + 16 * big, 16), pl.ds(128 * h, 128)]

    pack(out, piece)


def middle_kernel(pmsg, u_t, gate, v1, w2, msg, z1, prod, cells):
    unpack_one(pmsg, prod)
    v, w_next = v1[...], w2[...]
    for r in range(ROWS):
        out_bf = norm(row(prod, r).astype(F32))[0].astype(BF)
        state = row(u_t, r).astype(F32) + row(gate, r) * dot(v, out_bf, 0, 0)
        z1[pl.ds(r * C, C), :] = state
        operands(state, w_next, r, cells)
    pack_pair(msg, cells)


def cotangent_kernel(cot_t, z1, w2, v2, mix, grad_on, factors):
    w, v = w2[...], v2[...]
    for r in range(ROWS):
        nb = norm(row(z1, r))[0].astype(BF)
        grad_mix = (row(cot_t, r).astype(F32) * gate_of(nb, w)).astype(BF)
        mix[pl.ds(r * C, C), :] = grad_mix
        grad_on[pl.ds(r * C, C), :] = dot(v, grad_mix, 1, 0)
        store_factors(factors, r, gated(nb, w))


def turn_kernel(pmsg, grad_on, msg, prod, cells):
    unpack_one(pmsg, prod)
    for r in range(ROWS):
        normed, inv = norm(row(prod, r).astype(F32))
        cells[pl.ds(r * C, C), :] = norm_back(normed, inv, row(grad_on, r)).astype(BF)
    pack_one(msg, cells)


def gate_grads(grad_u, mix, prod, state, w, v):
    nb = norm(state)[0].astype(BF)
    gate = gate_of(nb, w)
    out_bf = norm(prod.astype(F32))[0].astype(BF)
    mixed = dot(v, out_bf, 0, 0)
    grad_gate = (grad_u * mixed * gate * (1.0 - gate)).astype(BF)
    return grad_gate, dot(out_bf, mix, 1, 1), dot(nb, grad_gate, 1, 1)


def late_kernel(grad_u, mix, prod, state, w_ref, v_ref, grad_gate, sums):
    w, v = w_ref[...], v_ref[...]
    grad_v = grad_w = 0.0
    for r in range(ROWS):
        gg, gv, gw = gate_grads(
            row(grad_u, r).astype(F32), row(mix, r), row(prod, r), row(state, r).astype(F32), w, v
        )
        grad_gate[pl.ds(r * C, C), :] = gg
        grad_v = grad_v + gv
        grad_w = grad_w + gw
    sums[pl.ds(0, C), :] = grad_w.astype(BF)
    sums[pl.ds(C, C), :] = grad_v.astype(BF)


def grads_kernel(incoming, gmsg, kept, msg, prod, sides):
    def put(q, big, rows):
        h, m, r = q // 8, (q // 4) % 2, q % 4
        prod[pl.ds(m * N + 64 * r + 16 * big, 16), pl.ds(128 * h, 128)] = rows

    unpack(gmsg, put)
    for m in range(2):
        left = kept[pl.ds(m * N, N), :]
        right = kept[pl.ds((2 + m) * N, N), :]
        grad = prod[pl.ds(m * N, N), :]
        if incoming:
            grad_left, grad_right = dot(right, grad, 1, 1), dot(left, grad, 1, 0)
        else:
            grad_left, grad_right = dot(grad, right, 1, 0), dot(grad, left, 0, 0)
        sides[pl.ds(m * N, N), :] = grad_left.astype(BF)
        sides[pl.ds((2 + m) * N, N), :] = grad_right.astype(BF)

    def piece(q, big):
        t, m, r = q // 8, (q // 4) % 2, q % 4
        return sides[pl.ds((2 * t + m) * N + 64 * r + 16 * big, 16), :]

    pack(msg, piece)


def project_grad(cells, r, factors):
    grad_left = cells[pl.ds(r * C, C), :].astype(F32)
    grad_right = cells[pl.ds((ROWS + r) * C, C), :].astype(F32)
    blocks = []
    for b, grad in enumerate((grad_left, grad_left, grad_right, grad_right)):
        blocks.append((grad * factors[pl.ds((4 * r + b) * C, C), :].astype(F32)).astype(BF))
    return jnp.concatenate(blocks, 0)


def input_grad(grad_u, normed, inv, grad_proj, grad_gate, w):
    grad = dot(w[:, : 4 * C], grad_proj, 1, 0) + dot(w[:, 4 * C :], grad_gate, 1, 0)
    return grad_u + norm_back(normed, inv, grad)


def back_kernel(
    gmsg, z1, gg2, cot_t, factors2, w2, gate1, prod1, v1, msg, proj, grad_u, mix, cells, grad_prod
):
    unpack_pair(gmsg, cells)
    w_in, v = w2[...], v1[...]
    for r in range(ROWS):
        normed, inv = norm(row(z1, r))
        grad_proj = project_grad(cells, r, factors2)
        proj[pl.ds(4 * r * C, 4 * C), :] = grad_proj
        grad = input_grad(row(cot_t, r).astype(F32), normed, inv, grad_proj, row(gg2, r), w_in)
        grad_u[pl.ds(r * C, C), :] = grad
        grad_mix = (grad * row(gate1, r)).astype(BF)
        mix[pl.ds(r * C, C), :] = grad_mix
        normed, inv = norm(row(prod1, r).astype(F32))
        grad_prod[pl.ds(r * C, C), :] = norm_back(normed, inv, dot(v, grad_mix, 1, 0)).astype(BF)
    pack_one(msg, grad_prod)


def weight_kernel(state, proj, sums):
    total = 0.0
    for r in range(ROWS):
        nb = norm(row(state, r).astype(F32))[0].astype(BF)
        total = total + dot(proj[pl.ds(4 * r * C, 4 * C), :], nb, 1, 1)
    sums[...] = total.astype(BF)


def last_kernel(gmsg, nb, factors1, lr2, gv2, gv1, msg, proj, cells):
    unpack_pair(gmsg, cells)
    total = 0.0
    for r in range(ROWS):
        grad_proj = project_grad(cells, r, factors1)
        proj[pl.ds(4 * r * C, 4 * C), :] = grad_proj
        total = total + dot(grad_proj, row(nb, r), 1, 1)
    msg[pl.ds(0, 4 * C), :] = total.astype(BF)
    msg[pl.ds(4 * C, 2 * C), :] = gv1[...]
    msg[pl.ds(6 * C, 4 * C), :] = lr2[...]
    msg[pl.ds(10 * C, 2 * C), :] = gv2[...]


def pair_kernel(u_t, proj, gg1, grad_u, w1, out):
    order = column_order()
    w = w1[...]
    for r in range(ROWS):
        normed, inv = norm(row(u_t, r).astype(F32))
        grad = input_grad(
            row(grad_u, r), normed, inv, proj[pl.ds(4 * r * C, 4 * C), :], row(gg1, r), w
        )
        out[r] = dot(order, grad.astype(BF), 0, 1).astype(BF)


def finish_kernel(sums, oi, oo, ii, io):
    for base, w, v in ((0, oi, oo), (6 * C, ii, io)):
        for b in range(4):
            w[:, pl.ds(b * C, C)] = sums[pl.ds(base + b * C, C), :].astype(F32).T
        w[:, pl.ds(4 * C, C)] = sums[pl.ds(base + 4 * C, C), :].astype(F32)
        v[...] = sums[pl.ds(base + 5 * C, C), :].astype(F32)


def call(kernel, outs, scratch, *args, name, flops=2e8, scalar=False):
    shapes = [jax.ShapeDtypeStruct(s, d) for s, d in outs]
    moved = sum(a.size * a.dtype.itemsize for a in args)
    moved += sum(s.size * s.dtype.itemsize for s in shapes)
    return pl.pallas_call(
        kernel,
        out_shape=shapes,
        in_specs=[
            pl.BlockSpec(memory_space=pltpu.SMEM if scalar and i == 0 else pltpu.VMEM)
            for i in range(len(args))
        ],
        scratch_shapes=[pltpu.VMEM(s, d) for s, d in scratch],
        compiler_params=pltpu.CompilerParams(vmem_limit_bytes=VMEM_LIMIT),
        cost_estimate=pl.CostEstimate(
            flops=int(flops), bytes_accessed=int(moved), transcendentals=0
        ),
        name=name,
    )(*args)


def exchange(msg):
    shape = msg.shape
    out = lax.all_to_all(msg.reshape(64, 16, shape[1]), "dap", 0, 0, tiled=True)
    return out.reshape(shape)


ONE = (ROWS * C, N)
TWO = (2 * ROWS * C, N)
ONE_MSG = (64 * 16, 128)
TWO_MSG = (64 * 16, 256)
PROJ = (4 * ROWS * C, N)


def product(msg, incoming):
    def kernel(*refs):
        product_kernel(incoming, *refs)

    return call(
        kernel, [((4 * N, N), BF), (ONE_MSG, BF)], [((2 * N, N), BF)], msg, name="product"
    )


def grads(gmsg, kept, incoming):
    def kernel(*refs):
        grads_kernel(incoming, *refs)

    return call(
        kernel, [(TWO_MSG, BF)], [((2 * N, N), BF), ((4 * N, N), BF)], gmsg, kept, name="grads"
    )[0]


def local(pair_act, cotangent, w1, v1, w2, v2):
    core = (lax.axis_index("rep") % 2).astype(jnp.int32).reshape(1)
    prepared = [(ONE, BF), (ONE, F32), (ONE, BF), (PROJ, BF)]
    lr1, u_t, *early = call(
        first_kernel,
        [(TWO_MSG, BF), (ONE, BF)] + prepared,
        [(TWO, BF)],
        core, pair_act[0], cotangent[0], w1,
        name="first",
        scalar=True,
    )
    cot_t, gate1, nb1, factors1 = call(
        second_kernel,
        prepared,
        [],
        core, u_t, cotangent[0], w1, *early,
        name="second",
        scalar=True,
    )
    kept1, pmsg1 = product(exchange(lr1), False)
    lr2, z1, prod1 = call(
        middle_kernel,
        [(TWO_MSG, BF), (ONE, F32), (ONE, BF)],
        [(TWO, BF)],
        exchange(pmsg1), u_t, gate1, v1, w2,
        name="middle",
    )
    mix2, grad_on2, factors2 = call(
        cotangent_kernel,
        [(ONE, BF), (ONE, F32), (PROJ, BF)],
        [],
        cot_t, z1, w2, v2,
        name="cotangent",
    )
    kept2, pmsg2 = product(exchange(lr2), True)
    gmsg2, prod2 = call(
        turn_kernel, [(ONE_MSG, BF), (ONE, BF)], [(ONE, BF)], exchange(pmsg2), grad_on2, name="turn"
    )
    gg2, gv2 = call(
        late_kernel,
        [(ONE, BF), ((2 * C, C), BF)],
        [],
        cot_t, mix2, prod2, z1, w2, v2,
        name="late_incoming",
    )
    gsides2 = grads(exchange(gmsg2), kept2, True)
    gmsg1, proj2, grad_u1, mix1 = call(
        back_kernel,
        [(ONE_MSG, BF), (PROJ, BF), (ONE, F32), (ONE, BF)],
        [(TWO, BF), (ONE, BF)],
        exchange(gsides2), z1, gg2, cot_t, factors2, w2, gate1, prod1, v1,
        name="back",
    )
    sums2 = call(weight_kernel, [((4 * C, C), BF)], [], z1, proj2, name="weights_incoming")[0]
    gg1, gv1 = call(
        late_kernel,
        [(ONE, BF), ((2 * C, C), BF)],
        [],
        grad_u1, mix1, prod1, u_t, w1, v1,
        name="late_outgoing",
    )
    gsides1 = grads(exchange(gmsg1), kept1, False)
    wmsg, proj1 = call(
        last_kernel,
        [((12 * C, C), BF), (PROJ, BF)],
        [(TWO, BF)],
        exchange(gsides1), nb1, factors1, sums2, gv2, gv1,
        name="last",
    )
    pair_grad = call(
        pair_kernel, [((ROWS, N, C), BF)], [], u_t, proj1, gg1, grad_u1, w1, name="pair"
    )[0]

    scale = 1.0 / math.sqrt(lax.axis_size("rep") * pair_act.shape[0] * N * N)
    parts = lax.all_to_all(wmsg.reshape(64, 24, C), "dap", 0, 0, tiled=True)
    part = jnp.sum(parts.astype(F32), axis=0)
    reps = lax.axis_size("rep")
    across = lax.all_to_all(jnp.broadcast_to(part, (reps, 24, C)), "rep", 0, 0, tiled=True)
    whole = (jnp.sum(across, axis=0) * scale).astype(BF)
    everywhere = lax.all_to_all(jnp.broadcast_to(whole, (64, 24, C)), "dap", 0, 0, tiled=True)
    oi, oo, ii, io = call(
        finish_kernel,
        [((C, 5 * C), F32), ((C, C), F32), ((C, 5 * C), F32), ((C, C), F32)],
        [],
        everywhere.reshape(12 * C, C),
        name="finish",
    )
    return pair_grad[None], oi, oo, ii, io


def solution(mesh):
    return jax.shard_map(
        local,
        mesh=mesh,
        in_specs=(P("rep", "dap", None, None), P("rep", "dap", None, None), P(), P(), P(), P()),
        out_specs=(P("rep", "dap", None, None), P(), P(), P(), P()),
        check_vma=False,
    )
```

```python
import math

import jax
import jax.numpy as jnp
from jax import lax
from jax.experimental import pallas as pl
from jax.experimental.pallas import tpu as pltpu
from jax.sharding import PartitionSpec as P

EPS = 1e-05
ROWS = 4
N = 256
C = 128
BF = jnp.bfloat16
F32 = jnp.float32
VMEM_LIMIT = 48 * 1024 * 1024


def dot(a, b, ca, cb):
    return lax.dot_general(a, b, (((ca,), (cb,)), ((), ())), preferred_element_type=F32)


def swap():
    row = lax.broadcasted_iota(jnp.int32, (256, 256), 0)
    col = lax.broadcasted_iota(jnp.int32, (256, 256), 1)
    hit = ((row & 15) == (col >> 4)) & ((row >> 4) == (col & 15))
    return jnp.where(hit, 1.0, 0.0).astype(BF)


def column_order():
    row = lax.broadcasted_iota(jnp.int32, (N, N), 0)
    col = lax.broadcasted_iota(jnp.int32, (N, N), 1)
    return jnp.where(col == 4 * (row & 63) + (row >> 6), 1.0, 0.0).astype(BF)


def norm(x):
    centred = x - jnp.mean(x, axis=0, keepdims=True)
    inv = lax.rsqrt(jnp.mean(centred * centred, axis=0, keepdims=True) + EPS)
    return centred * inv, inv


def norm_back(normed, inv, grad):
    first = jnp.mean(grad, axis=0, keepdims=True)
    second = jnp.mean(grad * normed, axis=0, keepdims=True)
    return inv * (grad - first - normed * second)


def pack(msg, piece):
    s = swap()
    for big in range(4):
        x = jnp.concatenate([piece(q, big) for q in range(16)], axis=0)
        msg[pl.ds(256 * big, 256), :] = dot(s, x, 1, 0).astype(BF)


def unpack(msg, put):
    s = swap()
    for big in range(4):
        y = dot(s, msg[pl.ds(256 * big, 256), :], 1, 0).astype(BF)
        for q in range(16):
            put(q, big, y[16 * q : 16 * q + 16, :])


def pack_pair(msg, cells):
    def piece(q, big):
        t, m, r = q // 8, (q // 4) % 2, q % 4
        return cells[pl.ds((t * ROWS + r) * C + m * 64 + 16 * big, 16), :]

    pack(msg, piece)


def unpack_pair(msg, cells):
    def put(q, big, rows):
        t, m, r = q // 8, (q // 4) % 2, q % 4
        cells[pl.ds((t * ROWS + r) * C + m * 64 + 16 * big, 16), :] = rows

    unpack(msg, put)


def pack_one(msg, cells):
    def piece(q, big):
        h, m, r = q // 8, (q // 4) % 2, q % 4
        return cells[pl.ds(r * C + m * 64 + 16 * big, 16), pl.ds(128 * h, 128)]

    pack(msg, piece)


def unpack_one(msg, cells):
    def put(q, big, rows):
        h, m, r = q // 8, (q // 4) % 2, q % 4
        cells[pl.ds(r * C + m * 64 + 16 * big, 16), pl.ds(128 * h, 128)] = rows

    unpack(msg, put)


def row(ref, r):
    return ref[pl.ds(r * C, C), :]


def gated(nb, w):
    pre = dot(w[:, : 4 * C], nb, 0, 0)
    return pre[:C], jax.nn.sigmoid(pre[C : 2 * C]), pre[2 * C : 3 * C], jax.nn.sigmoid(pre[3 * C :])


def gate_of(nb, w):
    return jax.nn.sigmoid(dot(w[:, 4 * C :], nb, 0, 0))


def operands(state, w, r, cells):
    normed, _ = norm(state)
    left, left_s, right, right_s = gated(normed.astype(BF), w)
    cells[pl.ds(r * C, C), :] = (left_s * left).astype(BF)
    cells[pl.ds((ROWS + r) * C, C), :] = (right_s * right).astype(BF)


def first_kernel(u, w1, turn, msg, u_t, cells):
    order = column_order()
    w = w1[...]
    for r in range(ROWS):
        state = dot(u[r], order, 0, 1)
        u_t[pl.ds(r * C, C), :] = state.astype(BF)
        operands(state, w, r, cells)
    pack_pair(msg, cells)


def product_kernel(incoming, msg, kept, out, prod):
    def put(q, big, rows):
        t, m, r = q // 8, (q // 4) % 2, q % 4
        kept[pl.ds((2 * t + m) * N + 64 * r + 16 * big, 16), :] = rows

    unpack(msg, put)
    over = 0 if incoming else 1
    for m in range(2):
        left = kept[pl.ds(m * N, N), :]
        right = kept[pl.ds((2 + m) * N, N), :]
        prod[pl.ds(m * N, N), :] = dot(left, right, over, over).astype(BF)

    def piece(q, big):
        h, m, r = q // 8, (q // 4) % 2, q % 4
        return prod[pl.ds(m * N + 64 * r + 16 * big, 16), pl.ds(128 * h, 128)]

    pack(out, piece)


def middle_kernel(pmsg, u_t, w1, v1, w2, msg, z1, prod, cells):
    unpack_one(pmsg, prod)
    w, v, w_next = w1[...], v1[...], w2[...]
    for r in range(ROWS):
        state = row(u_t, r).astype(F32)
        gate = gate_of(norm(state)[0].astype(BF), w)
        out_bf = norm(row(prod, r).astype(F32))[0].astype(BF)
        state = state + gate * dot(v, out_bf, 0, 0)
        z1[pl.ds(r * C, C), :] = state
        operands(state, w_next, r, cells)
    pack_pair(msg, cells)


def cotangent_kernel(cot, z1, w2, v2, cot_t, mix, grad_on):
    order = column_order()
    w, v = w2[...], v2[...]
    for r in range(ROWS):
        grad_u = dot(cot[r], order, 0, 1)
        cot_t[pl.ds(r * C, C), :] = grad_u.astype(BF)
        gate = gate_of(norm(row(z1, r))[0].astype(BF), w)
        grad_mix = (grad_u * gate).astype(BF)
        mix[pl.ds(r * C, C), :] = grad_mix
        grad_on[pl.ds(r * C, C), :] = dot(v, grad_mix, 1, 0)


def turn_kernel(pmsg, grad_on, msg, prod, cells):
    unpack_one(pmsg, prod)
    for r in range(ROWS):
        normed, inv = norm(row(prod, r).astype(F32))
        cells[pl.ds(r * C, C), :] = norm_back(normed, inv, row(grad_on, r)).astype(BF)
    pack_one(msg, cells)


def gate_grads(grad_u, mix, prod, state, w, v):
    nb = norm(state)[0].astype(BF)
    gate = gate_of(nb, w)
    out_bf = norm(prod.astype(F32))[0].astype(BF)
    mixed = dot(v, out_bf, 0, 0)
    grad_gate = (grad_u * mixed * gate * (1.0 - gate)).astype(BF)
    return grad_gate, dot(out_bf, mix, 1, 1), dot(nb, grad_gate, 1, 1)


def late_kernel(grad_u, mix, prod, state, w_ref, v_ref, grad_gate, sums):
    w, v = w_ref[...], v_ref[...]
    grad_v = grad_w = 0.0
    for r in range(ROWS):
        gg, gv, gw = gate_grads(
            row(grad_u, r).astype(F32), row(mix, r), row(prod, r), row(state, r).astype(F32), w, v
        )
        grad_gate[pl.ds(r * C, C), :] = gg
        grad_v = grad_v + gv
        grad_w = grad_w + gw
    sums[pl.ds(0, C), :] = grad_w.astype(BF)
    sums[pl.ds(C, C), :] = grad_v.astype(BF)


def grads_kernel(incoming, gmsg, kept, msg, prod, sides):
    def put(q, big, rows):
        h, m, r = q // 8, (q // 4) % 2, q % 4
        prod[pl.ds(m * N + 64 * r + 16 * big, 16), pl.ds(128 * h, 128)] = rows

    unpack(gmsg, put)
    for m in range(2):
        left = kept[pl.ds(m * N, N), :]
        right = kept[pl.ds((2 + m) * N, N), :]
        grad = prod[pl.ds(m * N, N), :]
        if incoming:
            grad_left, grad_right = dot(right, grad, 1, 1), dot(left, grad, 1, 0)
        else:
            grad_left, grad_right = dot(grad, right, 1, 0), dot(grad, left, 0, 0)
        sides[pl.ds(m * N, N), :] = grad_left.astype(BF)
        sides[pl.ds((2 + m) * N, N), :] = grad_right.astype(BF)

    def piece(q, big):
        t, m, r = q // 8, (q // 4) % 2, q % 4
        return sides[pl.ds((2 * t + m) * N + 64 * r + 16 * big, 16), :]

    pack(msg, piece)


def project_grad(cells, r, nb, w):
    left, left_s, right, right_s = gated(nb, w)
    grad_left = cells[pl.ds(r * C, C), :].astype(F32) * left_s
    grad_right = cells[pl.ds((ROWS + r) * C, C), :].astype(F32) * right_s
    return jnp.concatenate(
        [
            grad_left.astype(BF),
            (grad_left * left * (1.0 - left_s)).astype(BF),
            grad_right.astype(BF),
            (grad_right * right * (1.0 - right_s)).astype(BF),
        ],
        0,
    )


def input_grad(grad_u, normed, inv, grad_proj, grad_gate, w):
    grad = dot(w[:, : 4 * C], grad_proj, 1, 0) + dot(w[:, 4 * C :], grad_gate, 1, 0)
    return grad_u + norm_back(normed, inv, grad)


def back_kernel(
    gmsg, z1, gg2, cot_t, w2, u_t, prod1, w1, v1, msg, proj, grad_u, mix, cells, grad_prod
):
    unpack_pair(gmsg, cells)
    w_in, w, v = w2[...], w1[...], v1[...]
    for r in range(ROWS):
        normed, inv = norm(row(z1, r))
        grad_proj = project_grad(cells, r, normed.astype(BF), w_in)
        proj[pl.ds(4 * r * C, 4 * C), :] = grad_proj
        grad = input_grad(row(cot_t, r).astype(F32), normed, inv, grad_proj, row(gg2, r), w_in)
        grad_u[pl.ds(r * C, C), :] = grad
        gate = gate_of(norm(row(u_t, r).astype(F32))[0].astype(BF), w)
        grad_mix = (grad * gate).astype(BF)
        mix[pl.ds(r * C, C), :] = grad_mix
        normed, inv = norm(row(prod1, r).astype(F32))
        grad_prod[pl.ds(r * C, C), :] = norm_back(normed, inv, dot(v, grad_mix, 1, 0)).astype(BF)
    pack_one(msg, grad_prod)


def weight_kernel(state, proj, sums):
    total = 0.0
    for r in range(ROWS):
        nb = norm(row(state, r).astype(F32))[0].astype(BF)
        total = total + dot(proj[pl.ds(4 * r * C, 4 * C), :], nb, 1, 1)
    sums[...] = total.astype(BF)


def last_kernel(gmsg, u_t, w1, lr2, gv2, gv1, msg, proj, cells):
    unpack_pair(gmsg, cells)
    w = w1[...]
    total = 0.0
    for r in range(ROWS):
        nb = norm(row(u_t, r).astype(F32))[0].astype(BF)
        grad_proj = project_grad(cells, r, nb, w)
        proj[pl.ds(4 * r * C, 4 * C), :] = grad_proj
        total = total + dot(grad_proj, nb, 1, 1)
    msg[pl.ds(0, 4 * C), :] = total.astype(BF)
    msg[pl.ds(4 * C, 2 * C), :] = gv1[...]
    msg[pl.ds(6 * C, 4 * C), :] = lr2[...]
    msg[pl.ds(10 * C, 2 * C), :] = gv2[...]


def pair_kernel(u_t, proj, gg1, grad_u, w1, out):
    order = column_order()
    w = w1[...]
    for r in range(ROWS):
        normed, inv = norm(row(u_t, r).astype(F32))
        grad = input_grad(
            row(grad_u, r), normed, inv, proj[pl.ds(4 * r * C, 4 * C), :], row(gg1, r), w
        )
        out[r] = dot(order, grad.astype(BF), 0, 1).astype(BF)


def finish_kernel(sums, oi, oo, ii, io):
    for base, w, v in ((0, oi, oo), (6 * C, ii, io)):
        for b in range(4):
            w[:, pl.ds(b * C, C)] = sums[pl.ds(base + b * C, C), :].astype(F32).T
        w[:, pl.ds(4 * C, C)] = sums[pl.ds(base + 4 * C, C), :].astype(F32)
        v[...] = sums[pl.ds(base + 5 * C, C), :].astype(F32)


def call(kernel, outs, scratch, *args, name, flops=2e8):
    shapes = [jax.ShapeDtypeStruct(s, d) for s, d in outs]
    moved = sum(a.size * a.dtype.itemsize for a in args)
    moved += sum(s.size * s.dtype.itemsize for s in shapes)
    return pl.pallas_call(
        kernel,
        out_shape=shapes,
        scratch_shapes=[pltpu.VMEM(s, d) for s, d in scratch],
        compiler_params=pltpu.CompilerParams(vmem_limit_bytes=VMEM_LIMIT),
        cost_estimate=pl.CostEstimate(
            flops=int(flops), bytes_accessed=int(moved), transcendentals=0
        ),
        name=name,
    )(*args)


def exchange(msg):
    shape = msg.shape
    out = lax.all_to_all(msg.reshape(64, 16, shape[1]), "dap", 0, 0, tiled=True)
    return out.reshape(shape)


def stagger(pair_act):
    reps, devices = lax.axis_size("rep"), lax.axis_size("dap")
    pairs = [
        (rep * devices + d, rep * devices + (d ^ 4)) for rep in range(0, reps, 2) for d in range(devices)
    ]
    return lax.ppermute(pair_act[0, 0, :16], ("rep", "dap"), pairs)


ONE = (ROWS * C, N)
TWO = (2 * ROWS * C, N)
ONE_MSG = (64 * 16, 128)
TWO_MSG = (64 * 16, 256)
PROJ = (4 * ROWS * C, N)


def product(msg, incoming):
    def kernel(*refs):
        product_kernel(incoming, *refs)

    return call(
        kernel, [((4 * N, N), BF), (ONE_MSG, BF)], [((2 * N, N), BF)], msg, name="product"
    )


def grads(gmsg, kept, incoming):
    def kernel(*refs):
        grads_kernel(incoming, *refs)

    return call(
        kernel, [(TWO_MSG, BF)], [((2 * N, N), BF), ((4 * N, N), BF)], gmsg, kept, name="grads"
    )[0]


def local(pair_act, cotangent, w1, v1, w2, v2):
    lr1, u_t = call(
        first_kernel, [(TWO_MSG, BF), (ONE, BF)], [(TWO, BF)], pair_act[0], w1, stagger(pair_act), name="first"
    )
    kept1, pmsg1 = product(exchange(lr1), False)
    lr2, z1, prod1 = call(
        middle_kernel,
        [(TWO_MSG, BF), (ONE, F32), (ONE, BF)],
        [(TWO, BF)],
        exchange(pmsg1), u_t, w1, v1, w2,
        name="middle",
    )
    cot_t, mix2, grad_on2 = call(
        cotangent_kernel,
        [(ONE, BF), (ONE, BF), (ONE, F32)],
        [],
        cotangent[0], z1, w2, v2,
        name="cotangent",
    )
    kept2, pmsg2 = product(exchange(lr2), True)
    gmsg2, prod2 = call(
        turn_kernel, [(ONE_MSG, BF), (ONE, BF)], [(ONE, BF)], exchange(pmsg2), grad_on2, name="turn"
    )
    gg2, gv2 = call(
        late_kernel,
        [(ONE, BF), ((2 * C, C), BF)],
        [],
        cot_t, mix2, prod2, z1, w2, v2,
        name="late_incoming",
    )
    gsides2 = grads(exchange(gmsg2), kept2, True)
    gmsg1, proj2, grad_u1, mix1 = call(
        back_kernel,
        [(ONE_MSG, BF), (PROJ, BF), (ONE, F32), (ONE, BF)],
        [(TWO, BF), (ONE, BF)],
        exchange(gsides2), z1, gg2, cot_t, w2, u_t, prod1, w1, v1,
        name="back",
    )
    sums2 = call(weight_kernel, [((4 * C, C), BF)], [], z1, proj2, name="weights_incoming")[0]
    gg1, gv1 = call(
        late_kernel,
        [(ONE, BF), ((2 * C, C), BF)],
        [],
        grad_u1, mix1, prod1, u_t, w1, v1,
        name="late_outgoing",
    )
    gsides1 = grads(exchange(gmsg1), kept1, False)
    wmsg, proj1 = call(
        last_kernel,
        [((12 * C, C), BF), (PROJ, BF)],
        [(TWO, BF)],
        exchange(gsides1), u_t, w1, sums2, gv2, gv1,
        name="last",
    )
    pair_grad = call(
        pair_kernel, [((ROWS, N, C), BF)], [], u_t, proj1, gg1, grad_u1, w1, name="pair"
    )[0]

    scale = 1.0 / math.sqrt(lax.axis_size("rep") * pair_act.shape[0] * N * N)
    parts = lax.all_to_all(wmsg.reshape(64, 24, C), "dap", 0, 0, tiled=True)
    part = jnp.sum(parts.astype(F32), axis=0)
    reps = lax.axis_size("rep")
    across = lax.all_to_all(jnp.broadcast_to(part, (reps, 24, C)), "rep", 0, 0, tiled=True)
    whole = (jnp.sum(across, axis=0) * scale).astype(BF)
    everywhere = lax.all_to_all(jnp.broadcast_to(whole, (64, 24, C)), "dap", 0, 0, tiled=True)
    oi, oo, ii, io = call(
        finish_kernel,
        [((C, 5 * C), F32), ((C, C), F32), ((C, 5 * C), F32), ((C, C), F32)],
        [],
        everywhere.reshape(12 * C, C),
        name="finish",
    )
    return pair_grad[None], oi, oo, ii, io


def solution(mesh):
    return jax.shard_map(
        local,
        mesh=mesh,
        in_specs=(P("rep", "dap", None, None), P("rep", "dap", None, None), P(), P(), P(), P()),
        out_specs=(P("rep", "dap", None, None), P(), P(), P(), P()),
        check_vma=False,
    )
```

```python
import math

import jax
import jax.numpy as jnp
from jax import lax
from jax.experimental import pallas as pl
from jax.experimental.pallas import tpu as pltpu
from jax.sharding import PartitionSpec as P

EPS = 1e-05
ROWS = 4
N = 256
C = 128
BF = jnp.bfloat16
F32 = jnp.float32
VMEM_LIMIT = 48 * 1024 * 1024


def dot(a, b, ca, cb):
    return lax.dot_general(a, b, (((ca,), (cb,)), ((), ())), preferred_element_type=F32)


def swap():
    row = lax.broadcasted_iota(jnp.int32, (256, 256), 0)
    col = lax.broadcasted_iota(jnp.int32, (256, 256), 1)
    hit = ((row & 15) == (col >> 4)) & ((row >> 4) == (col & 15))
    return jnp.where(hit, 1.0, 0.0).astype(BF)


def column_order():
    row = lax.broadcasted_iota(jnp.int32, (N, N), 0)
    col = lax.broadcasted_iota(jnp.int32, (N, N), 1)
    return jnp.where(col == 4 * (row & 63) + (row >> 6), 1.0, 0.0).astype(BF)


def norm(x):
    centred = x - jnp.mean(x, axis=0, keepdims=True)
    inv = lax.rsqrt(jnp.mean(centred * centred, axis=0, keepdims=True) + EPS)
    return centred * inv, inv


def norm_back(normed, inv, grad):
    first = jnp.mean(grad, axis=0, keepdims=True)
    second = jnp.mean(grad * normed, axis=0, keepdims=True)
    return inv * (grad - first - normed * second)


def pack(msg, piece):
    s = swap()
    for big in range(4):
        x = jnp.concatenate([piece(q, big) for q in range(16)], axis=0)
        msg[pl.ds(256 * big, 256), :] = dot(s, x, 1, 0).astype(BF)


def unpack(msg, put):
    s = swap()
    for big in range(4):
        y = dot(s, msg[pl.ds(256 * big, 256), :], 1, 0).astype(BF)
        for q in range(16):
            put(q, big, y[16 * q : 16 * q + 16, :])


def pack_pair(msg, cells):
    def piece(q, big):
        t, m, r = q // 8, (q // 4) % 2, q % 4
        return cells[pl.ds((t * ROWS + r) * C + m * 64 + 16 * big, 16), :]

    pack(msg, piece)


def unpack_pair(msg, cells):
    def put(q, big, rows):
        t, m, r = q // 8, (q // 4) % 2, q % 4
        cells[pl.ds((t * ROWS + r) * C + m * 64 + 16 * big, 16), :] = rows

    unpack(msg, put)


def pack_one(msg, cells):
    def piece(q, big):
        h, m, r = q // 8, (q // 4) % 2, q % 4
        return cells[pl.ds(r * C + m * 64 + 16 * big, 16), pl.ds(128 * h, 128)]

    pack(msg, piece)


def unpack_one(msg, cells):
    def put(q, big, rows):
        h, m, r = q // 8, (q // 4) % 2, q % 4
        cells[pl.ds(r * C + m * 64 + 16 * big, 16), pl.ds(128 * h, 128)] = rows

    unpack(msg, put)


def row(ref, r):
    return ref[pl.ds(r * C, C), :]


def gated(nb, w):
    pre = dot(w[:, : 4 * C], nb, 0, 0)
    return pre[:C], jax.nn.sigmoid(pre[C : 2 * C]), pre[2 * C : 3 * C], jax.nn.sigmoid(pre[3 * C :])


def gate_of(nb, w):
    return jax.nn.sigmoid(dot(w[:, 4 * C :], nb, 0, 0))


def operands(state, w, r, cells):
    normed, _ = norm(state)
    left, left_s, right, right_s = gated(normed.astype(BF), w)
    cells[pl.ds(r * C, C), :] = (left_s * left).astype(BF)
    cells[pl.ds((ROWS + r) * C, C), :] = (right_s * right).astype(BF)


def first_kernel(u, w1, turn, msg, u_t, cells):
    order = column_order()
    w = w1[...]
    for r in range(ROWS):
        state = dot(u[r], order, 0, 1)
        u_t[pl.ds(r * C, C), :] = state.astype(BF)
        operands(state, w, r, cells)
    pack_pair(msg, cells)


def product_kernel(incoming, msg, kept, out, prod):
    def put(q, big, rows):
        t, m, r = q // 8, (q // 4) % 2, q % 4
        kept[pl.ds((2 * t + m) * N + 64 * r + 16 * big, 16), :] = rows

    unpack(msg, put)
    over = 0 if incoming else 1
    for m in range(2):
        left = kept[pl.ds(m * N, N), :]
        right = kept[pl.ds((2 + m) * N, N), :]
        prod[pl.ds(m * N, N), :] = dot(left, right, over, over).astype(BF)

    def piece(q, big):
        h, m, r = q // 8, (q // 4) % 2, q % 4
        return prod[pl.ds(m * N + 64 * r + 16 * big, 16), pl.ds(128 * h, 128)]

    pack(out, piece)


def middle_kernel(pmsg, u_t, w1, v1, w2, msg, z1, prod, cells):
    unpack_one(pmsg, prod)
    w, v, w_next = w1[...], v1[...], w2[...]
    for r in range(ROWS):
        state = row(u_t, r).astype(F32)
        gate = gate_of(norm(state)[0].astype(BF), w)
        out_bf = norm(row(prod, r).astype(F32))[0].astype(BF)
        state = state + gate * dot(v, out_bf, 0, 0)
        z1[pl.ds(r * C, C), :] = state
        operands(state, w_next, r, cells)
    pack_pair(msg, cells)


def cotangent_kernel(cot, z1, w2, v2, cot_t, mix, grad_on):
    order = column_order()
    w, v = w2[...], v2[...]
    for r in range(ROWS):
        grad_u = dot(cot[r], order, 0, 1)
        cot_t[pl.ds(r * C, C), :] = grad_u.astype(BF)
        gate = gate_of(norm(row(z1, r))[0].astype(BF), w)
        grad_mix = (grad_u * gate).astype(BF)
        mix[pl.ds(r * C, C), :] = grad_mix
        grad_on[pl.ds(r * C, C), :] = dot(v, grad_mix, 1, 0)


def turn_kernel(pmsg, grad_on, msg, prod, cells):
    unpack_one(pmsg, prod)
    for r in range(ROWS):
        normed, inv = norm(row(prod, r).astype(F32))
        cells[pl.ds(r * C, C), :] = norm_back(normed, inv, row(grad_on, r)).astype(BF)
    pack_one(msg, cells)


def gate_grads(grad_u, mix, prod, state, w, v):
    nb = norm(state)[0].astype(BF)
    gate = gate_of(nb, w)
    out_bf = norm(prod.astype(F32))[0].astype(BF)
    mixed = dot(v, out_bf, 0, 0)
    grad_gate = (grad_u * mixed * gate * (1.0 - gate)).astype(BF)
    return grad_gate, dot(out_bf, mix, 1, 1), dot(nb, grad_gate, 1, 1)


def late_kernel(grad_u, mix, prod, state, w_ref, v_ref, grad_gate, sums):
    w, v = w_ref[...], v_ref[...]
    grad_v = grad_w = 0.0
    for r in range(ROWS):
        gg, gv, gw = gate_grads(
            row(grad_u, r).astype(F32), row(mix, r), row(prod, r), row(state, r).astype(F32), w, v
        )
        grad_gate[pl.ds(r * C, C), :] = gg
        grad_v = grad_v + gv
        grad_w = grad_w + gw
    sums[pl.ds(0, C), :] = grad_w.astype(BF)
    sums[pl.ds(C, C), :] = grad_v.astype(BF)


def grads_kernel(incoming, gmsg, kept, turn, msg, prod, sides):
    def put(q, big, rows):
        h, m, r = q // 8, (q // 4) % 2, q % 4
        prod[pl.ds(m * N + 64 * r + 16 * big, 16), pl.ds(128 * h, 128)] = rows

    unpack(gmsg, put)
    for m in range(2):
        left = kept[pl.ds(m * N, N), :]
        right = kept[pl.ds((2 + m) * N, N), :]
        grad = prod[pl.ds(m * N, N), :]
        if incoming:
            grad_left, grad_right = dot(right, grad, 1, 1), dot(left, grad, 1, 0)
        else:
            grad_left, grad_right = dot(grad, right, 1, 0), dot(grad, left, 0, 0)
        sides[pl.ds(m * N, N), :] = grad_left.astype(BF)
        sides[pl.ds((2 + m) * N, N), :] = grad_right.astype(BF)

    def piece(q, big):
        t, m, r = q // 8, (q // 4) % 2, q % 4
        return sides[pl.ds((2 * t + m) * N + 64 * r + 16 * big, 16), :]

    pack(msg, piece)


def project_grad(cells, r, nb, w):
    left, left_s, right, right_s = gated(nb, w)
    grad_left = cells[pl.ds(r * C, C), :].astype(F32) * left_s
    grad_right = cells[pl.ds((ROWS + r) * C, C), :].astype(F32) * right_s
    return jnp.concatenate(
        [
            grad_left.astype(BF),
            (grad_left * left * (1.0 - left_s)).astype(BF),
            grad_right.astype(BF),
            (grad_right * right * (1.0 - right_s)).astype(BF),
        ],
        0,
    )


def input_grad(grad_u, normed, inv, grad_proj, grad_gate, w):
    grad = dot(w[:, : 4 * C], grad_proj, 1, 0) + dot(w[:, 4 * C :], grad_gate, 1, 0)
    return grad_u + norm_back(normed, inv, grad)


def back_kernel(
    gmsg, z1, gg2, cot_t, w2, u_t, prod1, w1, v1, msg, proj, grad_u, mix, cells, grad_prod
):
    unpack_pair(gmsg, cells)
    w_in, w, v = w2[...], w1[...], v1[...]
    for r in range(ROWS):
        normed, inv = norm(row(z1, r))
        grad_proj = project_grad(cells, r, normed.astype(BF), w_in)
        proj[pl.ds(4 * r * C, 4 * C), :] = grad_proj
        grad = input_grad(row(cot_t, r).astype(F32), normed, inv, grad_proj, row(gg2, r), w_in)
        grad_u[pl.ds(r * C, C), :] = grad
        gate = gate_of(norm(row(u_t, r).astype(F32))[0].astype(BF), w)
        grad_mix = (grad * gate).astype(BF)
        mix[pl.ds(r * C, C), :] = grad_mix
        normed, inv = norm(row(prod1, r).astype(F32))
        grad_prod[pl.ds(r * C, C), :] = norm_back(normed, inv, dot(v, grad_mix, 1, 0)).astype(BF)
    pack_one(msg, grad_prod)


def weight_kernel(state, proj, sums):
    total = 0.0
    for r in range(ROWS):
        nb = norm(row(state, r).astype(F32))[0].astype(BF)
        total = total + dot(proj[pl.ds(4 * r * C, 4 * C), :], nb, 1, 1)
    sums[...] = total.astype(BF)


def last_kernel(gmsg, u_t, w1, lr2, gv2, gv1, msg, proj, cells):
    unpack_pair(gmsg, cells)
    w = w1[...]
    total = 0.0
    for r in range(ROWS):
        nb = norm(row(u_t, r).astype(F32))[0].astype(BF)
        grad_proj = project_grad(cells, r, nb, w)
        proj[pl.ds(4 * r * C, 4 * C), :] = grad_proj
        total = total + dot(grad_proj, nb, 1, 1)
    msg[pl.ds(0, 4 * C), :] = total.astype(BF)
    msg[pl.ds(4 * C, 2 * C), :] = gv1[...]
    msg[pl.ds(6 * C, 4 * C), :] = lr2[...]
    msg[pl.ds(10 * C, 2 * C), :] = gv2[...]


def pair_kernel(u_t, proj, gg1, grad_u, w1, out):
    order = column_order()
    w = w1[...]
    for r in range(ROWS):
        normed, inv = norm(row(u_t, r).astype(F32))
        grad = input_grad(
            row(grad_u, r), normed, inv, proj[pl.ds(4 * r * C, 4 * C), :], row(gg1, r), w
        )
        out[r] = dot(order, grad.astype(BF), 0, 1).astype(BF)


def finish_kernel(sums, oi, oo, ii, io):
    for base, w, v in ((0, oi, oo), (6 * C, ii, io)):
        for b in range(4):
            w[:, pl.ds(b * C, C)] = sums[pl.ds(base + b * C, C), :].astype(F32).T
        w[:, pl.ds(4 * C, C)] = sums[pl.ds(base + 4 * C, C), :].astype(F32)
        v[...] = sums[pl.ds(base + 5 * C, C), :].astype(F32)


def call(kernel, outs, scratch, *args, name, flops=2e8, ordered=0):
    shapes = [jax.ShapeDtypeStruct(s, d) for s, d in outs]
    specs = [pl.BlockSpec(memory_space=pltpu.VMEM)] * (len(args) - ordered)
    specs += [pl.BlockSpec(memory_space=pl.ANY)] * ordered
    moved = sum(a.size * a.dtype.itemsize for a in args)
    moved += sum(s.size * s.dtype.itemsize for s in shapes)
    return pl.pallas_call(
        kernel,
        out_shape=shapes,
        in_specs=specs,
        scratch_shapes=[pltpu.VMEM(s, d) for s, d in scratch],
        compiler_params=pltpu.CompilerParams(vmem_limit_bytes=VMEM_LIMIT),
        cost_estimate=pl.CostEstimate(
            flops=int(flops), bytes_accessed=int(moved), transcendentals=0
        ),
        name=name,
    )(*args)


def exchange(msg):
    shape = msg.shape
    out = lax.all_to_all(msg.reshape(64, 16, shape[1]), "dap", 0, 0, tiled=True)
    return out.reshape(shape)


def pass_on(array, core):
    reps, devices = lax.axis_size("rep"), lax.axis_size("dap")
    pairs = [
        (rep * devices + d, rep * devices + (d ^ 4))
        for rep in range(core, reps, 2)
        for d in range(devices)
    ]
    return lax.ppermute(array, ("rep", "dap"), pairs)


ONE = (ROWS * C, N)
TWO = (2 * ROWS * C, N)
ONE_MSG = (64 * 16, 128)
TWO_MSG = (64 * 16, 256)
PROJ = (4 * ROWS * C, N)


def product(msg, incoming):
    def kernel(*refs):
        product_kernel(incoming, *refs)

    return call(
        kernel, [((4 * N, N), BF), (ONE_MSG, BF)], [((2 * N, N), BF)], msg, name="product"
    )


def grads(gmsg, kept, turn, incoming):
    def kernel(*refs):
        grads_kernel(incoming, *refs)

    return call(
        kernel, [(TWO_MSG, BF)], [((2 * N, N), BF), ((4 * N, N), BF)], gmsg, kept, turn, name="grads", ordered=1
    )[0]


def local(pair_act, cotangent, w1, v1, w2, v2):
    lr1, u_t = call(
        first_kernel, [(TWO_MSG, BF), (ONE, BF)], [(TWO, BF)], pair_act[0], w1, pass_on(v1, 0), name="first", ordered=1
    )
    kept1, pmsg1 = product(exchange(lr1), False)
    lr2, z1, prod1 = call(
        middle_kernel,
        [(TWO_MSG, BF), (ONE, F32), (ONE, BF)],
        [(TWO, BF)],
        exchange(pmsg1), u_t, w1, v1, w2,
        name="middle",
    )
    cot_t, mix2, grad_on2 = call(
        cotangent_kernel,
        [(ONE, BF), (ONE, BF), (ONE, F32)],
        [],
        cotangent[0], z1, w2, v2,
        name="cotangent",
    )
    kept2, pmsg2 = product(exchange(lr2), True)
    gmsg2, prod2 = call(
        turn_kernel, [(ONE_MSG, BF), (ONE, BF)], [(ONE, BF)], exchange(pmsg2), grad_on2, name="turn"
    )
    gg2, gv2 = call(
        late_kernel,
        [(ONE, BF), ((2 * C, C), BF)],
        [],
        cot_t, mix2, prod2, z1, w2, v2,
        name="late_incoming",
    )
    gsides2 = grads(exchange(gmsg2), kept2, v2, True)
    gmsg1, proj2, grad_u1, mix1 = call(
        back_kernel,
        [(ONE_MSG, BF), (PROJ, BF), (ONE, F32), (ONE, BF)],
        [(TWO, BF), (ONE, BF)],
        exchange(gsides2), z1, gg2, cot_t, w2, u_t, prod1, w1, v1,
        name="back",
    )
    sums2 = call(weight_kernel, [((4 * C, C), BF)], [], z1, proj2, name="weights_incoming")[0]
    gg1, gv1 = call(
        late_kernel,
        [(ONE, BF), ((2 * C, C), BF)],
        [],
        grad_u1, mix1, prod1, u_t, w1, v1,
        name="late_outgoing",
    )
    grad_ch = exchange(gmsg1)
    gsides1 = grads(grad_ch, kept1, pass_on(grad_ch, 1), False)
    wmsg, proj1 = call(
        last_kernel,
        [((12 * C, C), BF), (PROJ, BF)],
        [(TWO, BF)],
        exchange(gsides1), u_t, w1, sums2, gv2, gv1,
        name="last",
    )
    pair_grad = call(
        pair_kernel, [((ROWS, N, C), BF)], [], u_t, proj1, gg1, grad_u1, w1, name="pair"
    )[0]

    scale = 1.0 / math.sqrt(lax.axis_size("rep") * pair_act.shape[0] * N * N)
    parts = lax.all_to_all(wmsg.reshape(64, 24, C), "dap", 0, 0, tiled=True)
    part = jnp.sum(parts.astype(F32), axis=0)
    reps = lax.axis_size("rep")
    across = lax.all_to_all(jnp.broadcast_to(part, (reps, 24, C)), "rep", 0, 0, tiled=True)
    whole = (jnp.sum(across, axis=0) * scale).astype(BF)
    everywhere = lax.all_to_all(jnp.broadcast_to(whole, (64, 24, C)), "dap", 0, 0, tiled=True)
    oi, oo, ii, io = call(
        finish_kernel,
        [((C, 5 * C), F32), ((C, C), F32), ((C, 5 * C), F32), ((C, C), F32)],
        [],
        everywhere.reshape(12 * C, C),
        name="finish",
    )
    return pair_grad[None], oi, oo, ii, io


def solution(mesh):
    return jax.shard_map(
        local,
        mesh=mesh,
        in_specs=(P("rep", "dap", None, None), P("rep", "dap", None, None), P(), P(), P(), P()),
        out_specs=(P("rep", "dap", None, None), P(), P(), P(), P()),
        check_vma=False,
    )
```

```python
import math

import jax
import jax.numpy as jnp
from jax import lax
from jax.experimental import pallas as pl
from jax.experimental.pallas import tpu as pltpu
from jax.sharding import PartitionSpec as P

EPS = 1e-05
ROWS = 4
N = 256
C = 128
BF = jnp.bfloat16
F32 = jnp.float32
VMEM_LIMIT = 48 * 1024 * 1024


def dot(a, b, ca, cb):
    return lax.dot_general(a, b, (((ca,), (cb,)), ((), ())), preferred_element_type=F32)


def swap():
    row = lax.broadcasted_iota(jnp.int32, (256, 256), 0)
    col = lax.broadcasted_iota(jnp.int32, (256, 256), 1)
    hit = ((row & 15) == (col >> 4)) & ((row >> 4) == (col & 15))
    return jnp.where(hit, 1.0, 0.0).astype(BF)


def identity():
    row = lax.broadcasted_iota(jnp.int32, (N, N), 0)
    col = lax.broadcasted_iota(jnp.int32, (N, N), 1)
    return jnp.where(row == col, 1.0, 0.0).astype(BF)


def transposed(x):
    return dot(identity(), x, 1, 1).astype(BF)


def column_order():
    row = lax.broadcasted_iota(jnp.int32, (N, N), 0)
    col = lax.broadcasted_iota(jnp.int32, (N, N), 1)
    return jnp.where(col == 4 * (row & 63) + (row >> 6), 1.0, 0.0).astype(BF)


def norm(x):
    centred = x - jnp.mean(x, axis=0, keepdims=True)
    inv = lax.rsqrt(jnp.mean(centred * centred, axis=0, keepdims=True) + EPS)
    return centred * inv, inv


def norm_back(normed, inv, grad):
    first = jnp.mean(grad, axis=0, keepdims=True)
    second = jnp.mean(grad * normed, axis=0, keepdims=True)
    return inv * (grad - first - normed * second)


def pack(msg, piece):
    s = swap()
    for big in range(4):
        x = jnp.concatenate([piece(q, big) for q in range(16)], axis=0)
        msg[pl.ds(256 * big, 256), :] = dot(s, x, 1, 0).astype(BF)


def unpack(msg, put):
    s = swap()
    for big in range(4):
        y = dot(s, msg[pl.ds(256 * big, 256), :], 1, 0).astype(BF)
        for q in range(16):
            put(q, big, y[16 * q : 16 * q + 16, :])


def pack_pair(msg, cells):
    def piece(q, big):
        t, m, r = q // 8, (q // 4) % 2, q % 4
        return cells[pl.ds((t * ROWS + r) * C + m * 64 + 16 * big, 16), :]

    pack(msg, piece)


def unpack_pair(msg, cells):
    def put(q, big, rows):
        t, m, r = q // 8, (q // 4) % 2, q % 4
        cells[pl.ds((t * ROWS + r) * C + m * 64 + 16 * big, 16), :] = rows

    unpack(msg, put)


def pack_one(msg, cells):
    def piece(q, big):
        h, m, r = q // 8, (q // 4) % 2, q % 4
        return cells[pl.ds(r * C + m * 64 + 16 * big, 16), pl.ds(128 * h, 128)]

    pack(msg, piece)


def unpack_one(msg, cells):
    def put(q, big, rows):
        h, m, r = q // 8, (q // 4) % 2, q % 4
        cells[pl.ds(r * C + m * 64 + 16 * big, 16), pl.ds(128 * h, 128)] = rows

    unpack(msg, put)


def row(ref, r):
    return ref[pl.ds(r * C, C), :]


def gated(nb, w):
    pre = dot(w[:, : 4 * C], nb, 0, 0)
    return pre[:C], jax.nn.sigmoid(pre[C : 2 * C]), pre[2 * C : 3 * C], jax.nn.sigmoid(pre[3 * C :])


def gate_of(nb, w):
    return jax.nn.sigmoid(dot(w[:, 4 * C :], nb, 0, 0))


def operands(state, w, r, cells):
    normed, _ = norm(state)
    left, left_s, right, right_s = gated(normed.astype(BF), w)
    cells[pl.ds(r * C, C), :] = (left_s * left).astype(BF)
    cells[pl.ds((ROWS + r) * C, C), :] = (right_s * right).astype(BF)


def first_kernel(u_hbm, w_hbm, turn, msg, u_t, cells, u, w1, sems):
    loads = [
        pltpu.make_async_copy(u_hbm, u, sems.at[0]),
        pltpu.make_async_copy(w_hbm, w1, sems.at[1]),
    ]
    for load in loads:
        load.start()
    order = column_order()
    for load in loads:
        load.wait()
    w = w1[...]
    for r in range(ROWS):
        state = dot(u[r], order, 0, 1)
        u_t[pl.ds(r * C, C), :] = state.astype(BF)
        operands(state, w, r, cells)
    pack_pair(msg, cells)


def product_kernel(incoming, msg, kept, out, prod):
    def put(q, big, rows):
        t, m, r = q // 8, (q // 4) % 2, q % 4
        kept[pl.ds((2 * t + m) * N + 64 * r + 16 * big, 16), :] = rows

    unpack(msg, put)
    for m in range(2):
        left = kept[pl.ds(m * N, N), :]
        right = kept[pl.ds((2 + m) * N, N), :]
        if incoming:
            both = dot(transposed(left), right, 1, 0)
        else:
            both = dot(left, right, 1, 1)
        prod[pl.ds(m * N, N), :] = both.astype(BF)

    def piece(q, big):
        h, m, r = q // 8, (q // 4) % 2, q % 4
        return prod[pl.ds(m * N + 64 * r + 16 * big, 16), pl.ds(128 * h, 128)]

    pack(out, piece)


def middle_kernel(pmsg, u_t, w1, v1, w2, msg, z1, prod, cells):
    unpack_one(pmsg, prod)
    w, v, w_next = w1[...], v1[...], w2[...]
    for r in range(ROWS):
        state = row(u_t, r).astype(F32)
        gate = gate_of(norm(state)[0].astype(BF), w)
        out_bf = norm(row(prod, r).astype(F32))[0].astype(BF)
        state = state + gate * dot(v, out_bf, 0, 0)
        z1[pl.ds(r * C, C), :] = state
        operands(state, w_next, r, cells)
    pack_pair(msg, cells)


def cotangent_kernel(cot, z1, w2, v2, cot_t, mix, grad_on):
    order = column_order()
    w, v = w2[...], v2[...]
    for r in range(ROWS):
        grad_u = dot(cot[r], order, 0, 1)
        cot_t[pl.ds(r * C, C), :] = grad_u.astype(BF)
        gate = gate_of(norm(row(z1, r))[0].astype(BF), w)
        grad_mix = (grad_u * gate).astype(BF)
        mix[pl.ds(r * C, C), :] = grad_mix
        grad_on[pl.ds(r * C, C), :] = dot(v, grad_mix, 1, 0)


def turn_kernel(pmsg, grad_on, msg, prod, cells):
    unpack_one(pmsg, prod)
    for r in range(ROWS):
        normed, inv = norm(row(prod, r).astype(F32))
        cells[pl.ds(r * C, C), :] = norm_back(normed, inv, row(grad_on, r)).astype(BF)
    pack_one(msg, cells)


def gate_grads(grad_u, mix, prod, state, w, v):
    nb = norm(state)[0].astype(BF)
    gate = gate_of(nb, w)
    out_bf = norm(prod.astype(F32))[0].astype(BF)
    mixed = dot(v, out_bf, 0, 0)
    grad_gate = (grad_u * mixed * gate * (1.0 - gate)).astype(BF)
    return grad_gate, dot(out_bf, mix, 1, 1), dot(nb, grad_gate, 1, 1)


def late_kernel(grad_u, mix, prod, state, w_ref, v_ref, grad_gate, sums):
    w, v = w_ref[...], v_ref[...]
    grad_v = grad_w = 0.0
    for r in range(ROWS):
        gg, gv, gw = gate_grads(
            row(grad_u, r).astype(F32), row(mix, r), row(prod, r), row(state, r).astype(F32), w, v
        )
        grad_gate[pl.ds(r * C, C), :] = gg
        grad_v = grad_v + gv
        grad_w = grad_w + gw
    sums[pl.ds(0, C), :] = grad_w.astype(BF)
    sums[pl.ds(C, C), :] = grad_v.astype(BF)


def grads_kernel(incoming, gmsg, kept, turn, msg, prod, sides):
    def put(q, big, rows):
        h, m, r = q // 8, (q // 4) % 2, q % 4
        prod[pl.ds(m * N + 64 * r + 16 * big, 16), pl.ds(128 * h, 128)] = rows

    unpack(gmsg, put)
    for m in range(2):
        left = kept[pl.ds(m * N, N), :]
        right = kept[pl.ds((2 + m) * N, N), :]
        grad = prod[pl.ds(m * N, N), :]
        if incoming:
            grad_left, grad_right = dot(right, grad, 1, 1), dot(left, grad, 1, 0)
        else:
            grad_left, grad_right = dot(grad, right, 1, 0), dot(transposed(grad), left, 1, 0)
        sides[pl.ds(m * N, N), :] = grad_left.astype(BF)
        sides[pl.ds((2 + m) * N, N), :] = grad_right.astype(BF)

    def piece(q, big):
        t, m, r = q // 8, (q // 4) % 2, q % 4
        return sides[pl.ds((2 * t + m) * N + 64 * r + 16 * big, 16), :]

    pack(msg, piece)


def project_grad(cells, r, nb, w):
    left, left_s, right, right_s = gated(nb, w)
    grad_left = cells[pl.ds(r * C, C), :].astype(F32) * left_s
    grad_right = cells[pl.ds((ROWS + r) * C, C), :].astype(F32) * right_s
    return jnp.concatenate(
        [
            grad_left.astype(BF),
            (grad_left * left * (1.0 - left_s)).astype(BF),
            grad_right.astype(BF),
            (grad_right * right * (1.0 - right_s)).astype(BF),
        ],
        0,
    )


def input_grad(grad_u, normed, inv, grad_proj, grad_gate, w):
    grad = dot(w[:, : 4 * C], grad_proj, 1, 0) + dot(w[:, 4 * C :], grad_gate, 1, 0)
    return grad_u + norm_back(normed, inv, grad)


def back_kernel(
    gmsg, z1, gg2, cot_t, w2, u_t, prod1, w1, v1, msg, sums, grad_u, mix, cells, grad_prod
):
    unpack_pair(gmsg, cells)
    w_in, w, v = w2[...], w1[...], v1[...]
    total = 0.0
    for r in range(ROWS):
        normed, inv = norm(row(z1, r))
        nb = normed.astype(BF)
        grad_proj = project_grad(cells, r, nb, w_in)
        total = total + dot(nb, grad_proj, 1, 1)
        grad = input_grad(row(cot_t, r).astype(F32), normed, inv, grad_proj, row(gg2, r), w_in)
        grad_u[pl.ds(r * C, C), :] = grad
        gate = gate_of(norm(row(u_t, r).astype(F32))[0].astype(BF), w)
        grad_mix = (grad * gate).astype(BF)
        mix[pl.ds(r * C, C), :] = grad_mix
        normed, inv = norm(row(prod1, r).astype(F32))
        grad_prod[pl.ds(r * C, C), :] = norm_back(normed, inv, dot(v, grad_mix, 1, 0)).astype(BF)
    pack_one(msg, grad_prod)
    store_blocks(sums, total)


def store_blocks(sums, total):
    for b in range(4):
        sums[pl.ds(b * C, C), :] = total[:, b * C : (b + 1) * C].astype(BF)


def last_kernel(gmsg, u_t, w1, lr2, gv2, gv1, msg, proj, cells):
    unpack_pair(gmsg, cells)
    w = w1[...]
    total = 0.0
    for r in range(ROWS):
        nb = norm(row(u_t, r).astype(F32))[0].astype(BF)
        grad_proj = project_grad(cells, r, nb, w)
        proj[pl.ds(4 * r * C, 4 * C), :] = grad_proj
        total = total + dot(nb, grad_proj, 1, 1)
    store_blocks(msg, total)
    msg[pl.ds(4 * C, 2 * C), :] = gv1[...]
    msg[pl.ds(6 * C, 4 * C), :] = lr2[...]
    msg[pl.ds(10 * C, 2 * C), :] = gv2[...]


def pair_kernel(u_t, proj, gg1, grad_u, w1, out):
    order = column_order()
    w = w1[...]
    for r in range(ROWS):
        normed, inv = norm(row(u_t, r).astype(F32))
        grad = input_grad(
            row(grad_u, r), normed, inv, proj[pl.ds(4 * r * C, 4 * C), :], row(gg1, r), w
        )
        out[r] = dot(order, grad.astype(BF), 0, 1).astype(BF)


def finish_kernel(sums, oi, oo, ii, io):
    for base, w, v in ((0, oi, oo), (6 * C, ii, io)):
        for b in range(5):
            w[:, pl.ds(b * C, C)] = sums[pl.ds(base + b * C, C), :].astype(F32)
        v[...] = sums[pl.ds(base + 5 * C, C), :].astype(F32)


def call(kernel, outs, scratch, *args, name, flops=2e8, unread=0):
    shapes = [jax.ShapeDtypeStruct(s, d) for s, d in outs]
    specs = [pl.BlockSpec(memory_space=pltpu.VMEM)] * (len(args) - unread)
    specs += [pl.BlockSpec(memory_space=pl.ANY)] * unread
    moved = sum(a.size * a.dtype.itemsize for a in args)
    moved += sum(s.size * s.dtype.itemsize for s in shapes)
    return pl.pallas_call(
        kernel,
        out_shape=shapes,
        in_specs=specs,
        scratch_shapes=[pltpu.VMEM(*s) if isinstance(s, tuple) else s for s in scratch],
        compiler_params=pltpu.CompilerParams(vmem_limit_bytes=VMEM_LIMIT),
        cost_estimate=pl.CostEstimate(
            flops=int(flops), bytes_accessed=int(moved), transcendentals=0
        ),
        name=name,
    )(*args)


def exchange(msg):
    shape = msg.shape
    out = lax.all_to_all(msg.reshape(64, 16, shape[1]), "dap", 0, 0, tiled=True)
    return out.reshape(shape)


def pass_on(array, core):
    reps, devices = lax.axis_size("rep"), lax.axis_size("dap")
    pairs = [
        (rep * devices + d, rep * devices + (d ^ 4))
        for rep in range(core, reps, 2)
        for d in range(devices)
    ]
    return lax.ppermute(array, ("rep", "dap"), pairs)


ONE = (ROWS * C, N)
TWO = (2 * ROWS * C, N)
ONE_MSG = (64 * 16, 128)
TWO_MSG = (64 * 16, 256)
PROJ = (4 * ROWS * C, N)


def product(msg, incoming):
    def kernel(*refs):
        product_kernel(incoming, *refs)

    return call(
        kernel, [((4 * N, N), BF), (ONE_MSG, BF)], [((2 * N, N), BF)], msg, name="product"
    )


def grads(gmsg, kept, turn, incoming):
    def kernel(*refs):
        grads_kernel(incoming, *refs)

    return call(
        kernel, [(TWO_MSG, BF)], [((2 * N, N), BF), ((4 * N, N), BF)], gmsg, kept, turn, name="grads", unread=1
    )[0]


def local(pair_act, cotangent, w1, v1, w2, v2):
    lr1, u_t = call(
        first_kernel,
        [(TWO_MSG, BF), (ONE, BF)],
        [(TWO, BF), ((ROWS, N, C), BF), ((C, 5 * C), BF), pltpu.SemaphoreType.DMA((2,))],
        pair_act[0], w1, pass_on(v1, 0),
        name="first",
        unread=3,
    )
    kept1, pmsg1 = product(exchange(lr1), False)
    lr2, z1, prod1 = call(
        middle_kernel,
        [(TWO_MSG, BF), (ONE, F32), (ONE, BF)],
        [(TWO, BF)],
        exchange(pmsg1), u_t, w1, v1, w2,
        name="middle",
    )
    cot_t, mix2, grad_on2 = call(
        cotangent_kernel,
        [(ONE, BF), (ONE, BF), (ONE, F32)],
        [],
        cotangent[0], z1, w2, v2,
        name="cotangent",
    )
    kept2, pmsg2 = product(exchange(lr2), True)
    gmsg2, prod2 = call(
        turn_kernel, [(ONE_MSG, BF), (ONE, BF)], [(ONE, BF)], exchange(pmsg2), grad_on2, name="turn"
    )
    gg2, gv2 = call(
        late_kernel,
        [(ONE, BF), ((2 * C, C), BF)],
        [],
        cot_t, mix2, prod2, z1, w2, v2,
        name="late_incoming",
    )
    gsides2 = grads(exchange(gmsg2), kept2, v2, True)
    gmsg1, sums2, grad_u1, mix1 = call(
        back_kernel,
        [(ONE_MSG, BF), ((4 * C, C), BF), (ONE, F32), (ONE, BF)],
        [(TWO, BF), (ONE, BF)],
        exchange(gsides2), z1, gg2, cot_t, w2, u_t, prod1, w1, v1,
        name="back",
    )
    gg1, gv1 = call(
        late_kernel,
        [(ONE, BF), ((2 * C, C), BF)],
        [],
        grad_u1, mix1, prod1, u_t, w1, v1,
        name="late_outgoing",
    )
    grad_ch = exchange(gmsg1)
    gsides1 = grads(grad_ch, kept1, pass_on(grad_ch, 1), False)
    wmsg, proj1 = call(
        last_kernel,
        [((12 * C, C), BF), (PROJ, BF)],
        [(TWO, BF)],
        exchange(gsides1), u_t, w1, sums2, gv2, gv1,
        name="last",
    )
    pair_grad = call(
        pair_kernel, [((ROWS, N, C), BF)], [], u_t, proj1, gg1, grad_u1, w1, name="pair"
    )[0]

    scale = 1.0 / math.sqrt(lax.axis_size("rep") * pair_act.shape[0] * N * N)
    parts = lax.all_to_all(wmsg.reshape(64, 24, C), "dap", 0, 0, tiled=True)
    part = jnp.sum(parts.astype(F32), axis=0)
    reps = lax.axis_size("rep")
    across = lax.all_to_all(jnp.broadcast_to(part, (reps, 24, C)), "rep", 0, 0, tiled=True)
    whole = (jnp.sum(across, axis=0) * scale).astype(BF)
    everywhere = lax.all_to_all(jnp.broadcast_to(whole, (64, 24, C)), "dap", 0, 0, tiled=True)
    oi, oo, ii, io = call(
        finish_kernel,
        [((C, 5 * C), F32), ((C, C), F32), ((C, 5 * C), F32), ((C, C), F32)],
        [],
        everywhere.reshape(12 * C, C),
        name="finish",
    )
    return pair_grad[None], oi, oo, ii, io


def solution(mesh):
    return jax.shard_map(
        local,
        mesh=mesh,
        in_specs=(P("rep", "dap", None, None), P("rep", "dap", None, None), P(), P(), P(), P()),
        out_specs=(P("rep", "dap", None, None), P(), P(), P(), P()),
        check_vma=False,
    )
```

```python
import math

import jax
import jax.numpy as jnp
from jax import lax
from jax.experimental import pallas as pl
from jax.experimental.pallas import tpu as pltpu
from jax.sharding import PartitionSpec as P

EPS = 1e-05
ROWS = 4
N = 256
C = 128
BF = jnp.bfloat16
F32 = jnp.float32
VMEM_LIMIT = 48 * 1024 * 1024
VMEM_WHOLE = 60 * 1024 * 1024


def dot(a, b, ca, cb):
    return lax.dot_general(a, b, (((ca,), (cb,)), ((), ())), preferred_element_type=F32)


def swap():
    row = lax.broadcasted_iota(jnp.int32, (256, 256), 0)
    col = lax.broadcasted_iota(jnp.int32, (256, 256), 1)
    hit = ((row & 15) == (col >> 4)) & ((row >> 4) == (col & 15))
    return jnp.where(hit, 1.0, 0.0).astype(BF)


def column_order():
    row = lax.broadcasted_iota(jnp.int32, (N, N), 0)
    col = lax.broadcasted_iota(jnp.int32, (N, N), 1)
    return jnp.where(col == 4 * (row & 63) + (row >> 6), 1.0, 0.0).astype(BF)


def norm(x):
    centred = x - jnp.mean(x, axis=0, keepdims=True)
    inv = lax.rsqrt(jnp.mean(centred * centred, axis=0, keepdims=True) + EPS)
    return centred * inv, inv


def norm_back(normed, inv, grad):
    first = jnp.mean(grad, axis=0, keepdims=True)
    second = jnp.mean(grad * normed, axis=0, keepdims=True)
    return inv * (grad - first - normed * second)


def pack(msg, piece):
    s = swap()
    for big in range(4):
        x = jnp.concatenate([piece(q, big) for q in range(16)], axis=0)
        msg[pl.ds(256 * big, 256), :] = dot(s, x, 1, 0).astype(BF)


def unpack(msg, put):
    s = swap()
    for big in range(4):
        y = dot(s, msg[pl.ds(256 * big, 256), :], 1, 0).astype(BF)
        for q in range(16):
            put(q, big, y[16 * q : 16 * q + 16, :])


def pack_pair(msg, cells):
    def piece(q, big):
        t, m, r = q // 8, (q // 4) % 2, q % 4
        return cells[pl.ds((t * ROWS + r) * C + m * 64 + 16 * big, 16), :]

    pack(msg, piece)


def unpack_pair(msg, cells):
    def put(q, big, rows):
        t, m, r = q // 8, (q // 4) % 2, q % 4
        cells[pl.ds((t * ROWS + r) * C + m * 64 + 16 * big, 16), :] = rows

    unpack(msg, put)


def pack_one(msg, cells):
    def piece(q, big):
        h, m, r = q // 8, (q // 4) % 2, q % 4
        return cells[pl.ds(r * C + m * 64 + 16 * big, 16), pl.ds(128 * h, 128)]

    pack(msg, piece)


def unpack_one(msg, cells):
    def put(q, big, rows):
        h, m, r = q // 8, (q // 4) % 2, q % 4
        cells[pl.ds(r * C + m * 64 + 16 * big, 16), pl.ds(128 * h, 128)] = rows

    unpack(msg, put)


def row(ref, r):
    return ref[pl.ds(r * C, C), :]


def gated(nb, w):
    pre = dot(w[:, : 4 * C], nb, 0, 0)
    return pre[:C], jax.nn.sigmoid(pre[C : 2 * C]), pre[2 * C : 3 * C], jax.nn.sigmoid(pre[3 * C :])


def gate_of(nb, w):
    return jax.nn.sigmoid(dot(w[:, 4 * C :], nb, 0, 0))


def operands(state, w, r, cells):
    normed, _ = norm(state)
    left, left_s, right, right_s = gated(normed.astype(BF), w)
    cells[pl.ds(r * C, C), :] = (left_s * left).astype(BF)
    cells[pl.ds((ROWS + r) * C, C), :] = (right_s * right).astype(BF)


def first_kernel(u_hbm, w_hbm, msg, u_t, cells, u, w1, sems):
    loads = [
        pltpu.make_async_copy(u_hbm, u, sems.at[0]),
        pltpu.make_async_copy(w_hbm, w1, sems.at[1]),
    ]
    for load in loads:
        load.start()
    order = column_order()
    for load in loads:
        load.wait()
    w = w1[...]
    for r in range(ROWS):
        state = dot(u[r], order, 0, 1)
        u_t[pl.ds(r * C, C), :] = state.astype(BF)
        operands(state, w, r, cells)
    pack_pair(msg, cells)


def product_kernel(incoming, msg, kept, out, prod):
    def put(q, big, rows):
        t, m, r = q // 8, (q // 4) % 2, q % 4
        kept[pl.ds((2 * t + m) * N + 64 * r + 16 * big, 16), :] = rows

    unpack(msg, put)
    over = 0 if incoming else 1
    for m in range(2):
        left = kept[pl.ds(m * N, N), :]
        right = kept[pl.ds((2 + m) * N, N), :]
        prod[pl.ds(m * N, N), :] = dot(left, right, over, over).astype(BF)

    def piece(q, big):
        h, m, r = q // 8, (q // 4) % 2, q % 4
        return prod[pl.ds(m * N + 64 * r + 16 * big, 16), pl.ds(128 * h, 128)]

    pack(out, piece)


def middle_kernel(pmsg, u_t, w1, v1, w2, msg, z1, prod, cells):
    unpack_one(pmsg, prod)
    w, v, w_next = w1[...], v1[...], w2[...]
    for r in range(ROWS):
        state = row(u_t, r).astype(F32)
        gate = gate_of(norm(state)[0].astype(BF), w)
        out_bf = norm(row(prod, r).astype(F32))[0].astype(BF)
        state = state + gate * dot(v, out_bf, 0, 0)
        z1[pl.ds(r * C, C), :] = state
        operands(state, w_next, r, cells)
    pack_pair(msg, cells)


def cotangent_kernel(cot, z1, w2, v2, cot_t, mix, grad_on):
    order = column_order()
    w, v = w2[...], v2[...]
    for r in range(ROWS):
        grad_u = dot(cot[r], order, 0, 1)
        cot_t[pl.ds(r * C, C), :] = grad_u.astype(BF)
        gate = gate_of(norm(row(z1, r))[0].astype(BF), w)
        grad_mix = (grad_u * gate).astype(BF)
        mix[pl.ds(r * C, C), :] = grad_mix
        grad_on[pl.ds(r * C, C), :] = dot(v, grad_mix, 1, 0)


def turn_kernel(pmsg, grad_on, msg, prod, cells):
    unpack_one(pmsg, prod)
    for r in range(ROWS):
        normed, inv = norm(row(prod, r).astype(F32))
        cells[pl.ds(r * C, C), :] = norm_back(normed, inv, row(grad_on, r)).astype(BF)
    pack_one(msg, cells)


def gate_grads(grad_u, mix, prod, state, w, v):
    nb = norm(state)[0].astype(BF)
    gate = gate_of(nb, w)
    out_bf = norm(prod.astype(F32))[0].astype(BF)
    mixed = dot(v, out_bf, 0, 0)
    grad_gate = (grad_u * mixed * gate * (1.0 - gate)).astype(BF)
    return grad_gate, dot(out_bf, mix, 1, 1), dot(nb, grad_gate, 1, 1)


def late_kernel(grad_u, mix, prod, state, w_ref, v_ref, grad_gate, sums):
    w, v = w_ref[...], v_ref[...]
    grad_v = grad_w = 0.0
    for r in range(ROWS):
        gg, gv, gw = gate_grads(
            row(grad_u, r).astype(F32), row(mix, r), row(prod, r), row(state, r).astype(F32), w, v
        )
        grad_gate[pl.ds(r * C, C), :] = gg
        grad_v = grad_v + gv
        grad_w = grad_w + gw
    sums[pl.ds(0, C), :] = grad_w.astype(BF)
    sums[pl.ds(C, C), :] = grad_v.astype(BF)


def grads_kernel(incoming, gmsg, kept, turn, msg, prod, sides):
    def put(q, big, rows):
        h, m, r = q // 8, (q // 4) % 2, q % 4
        prod[pl.ds(m * N + 64 * r + 16 * big, 16), pl.ds(128 * h, 128)] = rows

    unpack(gmsg, put)
    for m in range(2):
        left = kept[pl.ds(m * N, N), :]
        right = kept[pl.ds((2 + m) * N, N), :]
        grad = prod[pl.ds(m * N, N), :]
        if incoming:
            grad_left, grad_right = dot(right, grad, 1, 1), dot(left, grad, 1, 0)
        else:
            grad_left, grad_right = dot(grad, right, 1, 0), dot(grad, left, 0, 0)
        sides[pl.ds(m * N, N), :] = grad_left.astype(BF)
        sides[pl.ds((2 + m) * N, N), :] = grad_right.astype(BF)

    def piece(q, big):
        t, m, r = q // 8, (q // 4) % 2, q % 4
        return sides[pl.ds((2 * t + m) * N + 64 * r + 16 * big, 16), :]

    pack(msg, piece)


def project_grad(cells, r, nb, w):
    left, left_s, right, right_s = gated(nb, w)
    grad_left = cells[pl.ds(r * C, C), :].astype(F32) * left_s
    grad_right = cells[pl.ds((ROWS + r) * C, C), :].astype(F32) * right_s
    return jnp.concatenate(
        [
            grad_left.astype(BF),
            (grad_left * left * (1.0 - left_s)).astype(BF),
            grad_right.astype(BF),
            (grad_right * right * (1.0 - right_s)).astype(BF),
        ],
        0,
    )


def input_grad(grad_u, normed, inv, grad_proj, grad_gate, w):
    grad = dot(w[:, : 4 * C], grad_proj, 1, 0) + dot(w[:, 4 * C :], grad_gate, 1, 0)
    return grad_u + norm_back(normed, inv, grad)


def back_kernel(
    gmsg, z1, gg2, cot_t, w2, u_t, prod1, w1, v1, msg, sums, grad_u, mix, cells, grad_prod
):
    unpack_pair(gmsg, cells)
    w_in, w, v = w2[...], w1[...], v1[...]
    total = 0.0
    for r in range(ROWS):
        normed, inv = norm(row(z1, r))
        nb = normed.astype(BF)
        grad_proj = project_grad(cells, r, nb, w_in)
        total = total + dot(grad_proj, nb, 1, 1)
        grad = input_grad(row(cot_t, r).astype(F32), normed, inv, grad_proj, row(gg2, r), w_in)
        grad_u[pl.ds(r * C, C), :] = grad
        gate = gate_of(norm(row(u_t, r).astype(F32))[0].astype(BF), w)
        grad_mix = (grad * gate).astype(BF)
        mix[pl.ds(r * C, C), :] = grad_mix
        normed, inv = norm(row(prod1, r).astype(F32))
        grad_prod[pl.ds(r * C, C), :] = norm_back(normed, inv, dot(v, grad_mix, 1, 0)).astype(BF)
    pack_one(msg, grad_prod)
    sums[...] = total.astype(BF)


def last_kernel(gmsg, u_t, w1, lr2, gv2, gv1, msg, proj, cells):
    unpack_pair(gmsg, cells)
    w = w1[...]
    total = 0.0
    for r in range(ROWS):
        nb = norm(row(u_t, r).astype(F32))[0].astype(BF)
        grad_proj = project_grad(cells, r, nb, w)
        proj[pl.ds(4 * r * C, 4 * C), :] = grad_proj
        total = total + dot(grad_proj, nb, 1, 1)
    msg[pl.ds(0, 4 * C), :] = total.astype(BF)
    msg[pl.ds(4 * C, 2 * C), :] = gv1[...]
    msg[pl.ds(6 * C, 4 * C), :] = lr2[...]
    msg[pl.ds(10 * C, 2 * C), :] = gv2[...]


def pair_kernel(u_t, proj, gg1, grad_u, w1, out):
    order = column_order()
    w = w1[...]
    for r in range(ROWS):
        normed, inv = norm(row(u_t, r).astype(F32))
        grad = input_grad(
            row(grad_u, r), normed, inv, proj[pl.ds(4 * r * C, 4 * C), :], row(gg1, r), w
        )
        out[r] = dot(order, grad.astype(BF), 0, 1).astype(BF)


def finish_kernel(sums, oi, oo, ii, io):
    for base, w, v in ((0, oi, oo), (6 * C, ii, io)):
        for b in range(4):
            w[:, pl.ds(b * C, C)] = sums[pl.ds(base + b * C, C), :].astype(F32).T
        w[:, pl.ds(4 * C, C)] = sums[pl.ds(base + 4 * C, C), :].astype(F32)
        v[...] = sums[pl.ds(base + 5 * C, C), :].astype(F32)


def call(kernel, outs, scratch, *args, name, place=pl.ANY, placed=0, vmem=VMEM_LIMIT):
    shapes = [jax.ShapeDtypeStruct(s, d) for s, d in outs]
    specs = [pl.BlockSpec(memory_space=pltpu.VMEM)] * (len(args) - placed)
    specs += [pl.BlockSpec(memory_space=place)] * placed
    moved = sum(a.size * a.dtype.itemsize for a in args)
    moved += sum(s.size * s.dtype.itemsize for s in shapes)
    return pl.pallas_call(
        kernel,
        out_shape=shapes,
        in_specs=specs,
        scratch_shapes=[pltpu.VMEM(*s) if isinstance(s, tuple) else s for s in scratch],
        compiler_params=pltpu.CompilerParams(vmem_limit_bytes=vmem),
        cost_estimate=pl.CostEstimate(
            flops=200_000_000, bytes_accessed=int(moved), transcendentals=0
        ),
        name=name,
    )(*args)


def exchange(msg):
    shape = msg.shape
    out = lax.all_to_all(msg.reshape(64, 16, shape[1]), "dap", 0, 0, tiled=True)
    return out.reshape(shape)


def pass_on(array, core):
    reps, devices = lax.axis_size("rep"), lax.axis_size("dap")
    pairs = [
        (rep * devices + d, rep * devices + (d ^ 4))
        for rep in range(core, reps, 2)
        for d in range(devices)
    ]
    return lax.ppermute(array, ("rep", "dap"), pairs)


def after(msg, turn):
    def kernel(old, turn, new):
        pass

    return pl.pallas_call(
        kernel,
        out_shape=jax.ShapeDtypeStruct(msg.shape, msg.dtype),
        in_specs=[pl.BlockSpec(memory_space=pl.ANY)] * 2,
        out_specs=pl.BlockSpec(memory_space=pl.ANY),
        input_output_aliases={0: 0},
        compiler_params=pltpu.CompilerParams(vmem_limit_bytes=VMEM_WHOLE),
        name="after",
    )(msg, turn)


ONE = (ROWS * C, N)
TWO = (2 * ROWS * C, N)
ONE_MSG = (64 * 16, 128)
TWO_MSG = (64 * 16, 256)
PROJ = (4 * ROWS * C, N)


def product(msg, incoming):
    def kernel(*refs):
        product_kernel(incoming, *refs)

    return call(
        kernel, [((4 * N, N), BF), (ONE_MSG, BF)], [((2 * N, N), BF)], msg, name="product"
    )


def grads(gmsg, kept, turn, incoming):
    def kernel(*refs):
        grads_kernel(incoming, *refs)

    return call(
        kernel, [(TWO_MSG, BF)], [((2 * N, N), BF), ((4 * N, N), BF)], gmsg, kept, turn, name="grads", placed=1
    )[0]


def local(pair_act, cotangent, w1, v1, w2, v2):
    lr1, u_t = call(
        first_kernel,
        [(TWO_MSG, BF), (ONE, BF)],
        [(TWO, BF), ((ROWS, N, C), BF), ((C, 5 * C), BF), pltpu.SemaphoreType.DMA((2,))],
        pair_act[0], w1,
        name="first",
        place=pltpu.HBM,
        placed=2,
        vmem=VMEM_WHOLE,
    )
    kept1, pmsg1 = product(exchange(after(lr1, pass_on(w1, 0))), False)
    lr2, z1, prod1 = call(
        middle_kernel,
        [(TWO_MSG, BF), (ONE, F32), (ONE, BF)],
        [(TWO, BF)],
        exchange(pmsg1), u_t, w1, v1, w2,
        name="middle",
    )
    cot_t, mix2, grad_on2 = call(
        cotangent_kernel,
        [(ONE, BF), (ONE, BF), (ONE, F32)],
        [],
        cotangent[0], z1, w2, v2,
        name="cotangent",
    )
    kept2, pmsg2 = product(exchange(lr2), True)
    gmsg2, prod2 = call(
        turn_kernel, [(ONE_MSG, BF), (ONE, BF)], [(ONE, BF)], exchange(pmsg2), grad_on2, name="turn"
    )
    gg2, gv2 = call(
        late_kernel,
        [(ONE, BF), ((2 * C, C), BF)],
        [],
        cot_t, mix2, prod2, z1, w2, v2,
        name="late_incoming",
    )
    gsides2 = grads(exchange(gmsg2), kept2, v2, True)
    gmsg1, sums2, grad_u1, mix1 = call(
        back_kernel,
        [(ONE_MSG, BF), ((4 * C, C), BF), (ONE, F32), (ONE, BF)],
        [(TWO, BF), (ONE, BF)],
        exchange(gsides2), z1, gg2, cot_t, w2, u_t, prod1, w1, v1,
        name="back",
    )
    gg1, gv1 = call(
        late_kernel,
        [(ONE, BF), ((2 * C, C), BF)],
        [],
        grad_u1, mix1, prod1, u_t, w1, v1,
        name="late_outgoing",
    )
    grad_ch = exchange(gmsg1)
    gsides1 = grads(grad_ch, kept1, pass_on(grad_ch, 1), False)
    wmsg, proj1 = call(
        last_kernel,
        [((12 * C, C), BF), (PROJ, BF)],
        [(TWO, BF)],
        exchange(gsides1), u_t, w1, sums2, gv2, gv1,
        name="last",
    )
    pair_grad = call(
        pair_kernel, [((ROWS, N, C), BF)], [], u_t, proj1, gg1, grad_u1, w1, name="pair"
    )[0]

    scale = 1.0 / math.sqrt(lax.axis_size("rep") * pair_act.shape[0] * N * N)
    parts = lax.all_to_all(wmsg.reshape(64, 24, C), "dap", 0, 0, tiled=True)
    part = jnp.sum(parts.astype(F32), axis=0)
    reps = lax.axis_size("rep")
    across = lax.all_to_all(jnp.broadcast_to(part, (reps, 24, C)), "rep", 0, 0, tiled=True)
    whole = (jnp.sum(across, axis=0) * scale).astype(BF)
    everywhere = lax.all_to_all(jnp.broadcast_to(whole, (64, 24, C)), "dap", 0, 0, tiled=True)
    oi, oo, ii, io = call(
        finish_kernel,
        [((C, 5 * C), F32), ((C, C), F32), ((C, 5 * C), F32), ((C, C), F32)],
        [],
        everywhere.reshape(12 * C, C),
        name="finish",
    )
    return pair_grad[None], oi, oo, ii, io


def solution(mesh):
    return jax.shard_map(
        local,
        mesh=mesh,
        in_specs=(P("rep", "dap", None, None), P("rep", "dap", None, None), P(), P(), P(), P()),
        out_specs=(P("rep", "dap", None, None), P(), P(), P(), P()),
        check_vma=False,
    )
```

```python
import math

import jax
import jax.numpy as jnp
from jax import lax
from jax.experimental import pallas as pl
from jax.experimental.pallas import tpu as pltpu
from jax.sharding import PartitionSpec as P

EPS = 1e-05
ROWS = 4
N = 256
C = 128
BF = jnp.bfloat16
F32 = jnp.float32
VMEM_LIMIT = 48 * 1024 * 1024


def dot(a, b, ca, cb):
    return lax.dot_general(a, b, (((ca,), (cb,)), ((), ())), preferred_element_type=F32)


def swap():
    row = lax.broadcasted_iota(jnp.int32, (256, 256), 0)
    col = lax.broadcasted_iota(jnp.int32, (256, 256), 1)
    hit = ((row & 15) == (col >> 4)) & ((row >> 4) == (col & 15))
    return jnp.where(hit, 1.0, 0.0).astype(BF)


def column_order():
    row = lax.broadcasted_iota(jnp.int32, (N, N), 0)
    col = lax.broadcasted_iota(jnp.int32, (N, N), 1)
    return jnp.where(col == 4 * (row & 63) + (row >> 6), 1.0, 0.0).astype(BF)


def norm(x):
    centred = x - jnp.mean(x, axis=0, keepdims=True)
    inv = lax.rsqrt(jnp.mean(centred * centred, axis=0, keepdims=True) + EPS)
    return centred * inv, inv


def norm_back(normed, inv, grad):
    first = jnp.mean(grad, axis=0, keepdims=True)
    second = jnp.mean(grad * normed, axis=0, keepdims=True)
    return inv * (grad - first - normed * second)


def pack(msg, piece):
    s = swap()
    for big in range(4):
        x = jnp.concatenate([piece(q, big) for q in range(16)], axis=0)
        msg[pl.ds(256 * big, 256), :] = dot(s, x, 1, 0).astype(BF)


def unpack(msg, put):
    s = swap()
    for big in range(4):
        y = dot(s, msg[pl.ds(256 * big, 256), :], 1, 0).astype(BF)
        for q in range(16):
            put(q, big, y[16 * q : 16 * q + 16, :])


def pack_pair(msg, cells):
    def piece(q, big):
        t, m, r = q // 8, (q // 4) % 2, q % 4
        return cells[pl.ds((t * ROWS + r) * C + m * 64 + 16 * big, 16), :]

    pack(msg, piece)


def unpack_pair(msg, cells):
    def put(q, big, rows):
        t, m, r = q // 8, (q // 4) % 2, q % 4
        cells[pl.ds((t * ROWS + r) * C + m * 64 + 16 * big, 16), :] = rows

    unpack(msg, put)


def pack_one(msg, cells):
    def piece(q, big):
        h, m, r = q // 8, (q // 4) % 2, q % 4
        return cells[pl.ds(r * C + m * 64 + 16 * big, 16), pl.ds(128 * h, 128)]

    pack(msg, piece)


def unpack_one(msg, cells):
    def put(q, big, rows):
        h, m, r = q // 8, (q // 4) % 2, q % 4
        cells[pl.ds(r * C + m * 64 + 16 * big, 16), pl.ds(128 * h, 128)] = rows

    unpack(msg, put)


def row(ref, r):
    return ref[pl.ds(r * C, C), :]


def gated(nb, w):
    pre = dot(w[:, : 4 * C], nb, 0, 0)
    return pre[:C], jax.nn.sigmoid(pre[C : 2 * C]), pre[2 * C : 3 * C], jax.nn.sigmoid(pre[3 * C :])


def gate_of(nb, w):
    return jax.nn.sigmoid(dot(w[:, 4 * C :], nb, 0, 0))


def operands(state, w, r, cells):
    normed, _ = norm(state)
    left, left_s, right, right_s = gated(normed.astype(BF), w)
    cells[pl.ds(r * C, C), :] = (left_s * left).astype(BF)
    cells[pl.ds((ROWS + r) * C, C), :] = (right_s * right).astype(BF)


def first_kernel(u, w1, turn, msg, u_t, cells):
    order = column_order()
    w = w1[...]
    for r in range(ROWS):
        state = dot(u[r], order, 0, 1)
        u_t[pl.ds(r * C, C), :] = state.astype(BF)
        operands(state, w, r, cells)
    pack_pair(msg, cells)


def product_kernel(incoming, msg, kept, out, prod):
    def put(q, big, rows):
        t, m, r = q // 8, (q // 4) % 2, q % 4
        kept[pl.ds((2 * t + m) * N + 64 * r + 16 * big, 16), :] = rows

    unpack(msg, put)
    over = 0 if incoming else 1
    for m in range(2):
        left = kept[pl.ds(m * N, N), :]
        right = kept[pl.ds((2 + m) * N, N), :]
        prod[pl.ds(m * N, N), :] = dot(left, right, over, over).astype(BF)

    def piece(q, big):
        h, m, r = q // 8, (q // 4) % 2, q % 4
        return prod[pl.ds(m * N + 64 * r + 16 * big, 16), pl.ds(128 * h, 128)]

    pack(out, piece)


def middle_kernel(pmsg, u_t, w1, v1, w2, msg, z1, prod, cells):
    unpack_one(pmsg, prod)
    w, v, w_next = w1[...], v1[...], w2[...]
    for r in range(ROWS):
        state = row(u_t, r).astype(F32)
        gate = gate_of(norm(state)[0].astype(BF), w)
        out_bf = norm(row(prod, r).astype(F32))[0].astype(BF)
        state = state + gate * dot(v, out_bf, 0, 0)
        z1[pl.ds(r * C, C), :] = state
        operands(state, w_next, r, cells)
    pack_pair(msg, cells)


def cotangent_kernel(cot, z1, w2, v2, cot_t, mix, grad_on):
    order = column_order()
    w, v = w2[...], v2[...]
    for r in range(ROWS):
        grad_u = dot(cot[r], order, 0, 1)
        cot_t[pl.ds(r * C, C), :] = grad_u.astype(BF)
        gate = gate_of(norm(row(z1, r))[0].astype(BF), w)
        grad_mix = (grad_u * gate).astype(BF)
        mix[pl.ds(r * C, C), :] = grad_mix
        grad_on[pl.ds(r * C, C), :] = dot(v, grad_mix, 1, 0)


def turn_kernel(pmsg, grad_on, msg, prod, cells):
    unpack_one(pmsg, prod)
    for r in range(ROWS):
        normed, inv = norm(row(prod, r).astype(F32))
        cells[pl.ds(r * C, C), :] = norm_back(normed, inv, row(grad_on, r)).astype(BF)
    pack_one(msg, cells)


def gate_grads(grad_u, mix, prod, state, w, v):
    nb = norm(state)[0].astype(BF)
    gate = gate_of(nb, w)
    out_bf = norm(prod.astype(F32))[0].astype(BF)
    mixed = dot(v, out_bf, 0, 0)
    grad_gate = (grad_u * mixed * gate * (1.0 - gate)).astype(BF)
    return grad_gate, dot(out_bf, mix, 1, 1), dot(nb, grad_gate, 1, 1)


def late_kernel(grad_u, mix, prod, state, w_ref, v_ref, grad_gate, sums):
    w, v = w_ref[...], v_ref[...]
    grad_v = grad_w = 0.0
    for r in range(ROWS):
        gg, gv, gw = gate_grads(
            row(grad_u, r).astype(F32), row(mix, r), row(prod, r), row(state, r).astype(F32), w, v
        )
        grad_gate[pl.ds(r * C, C), :] = gg
        grad_v = grad_v + gv
        grad_w = grad_w + gw
    sums[pl.ds(0, C), :] = grad_w.astype(BF)
    sums[pl.ds(C, C), :] = grad_v.astype(BF)


def grads_kernel(incoming, gmsg, kept, msg, prod, sides):
    def put(q, big, rows):
        h, m, r = q // 8, (q // 4) % 2, q % 4
        prod[pl.ds(m * N + 64 * r + 16 * big, 16), pl.ds(128 * h, 128)] = rows

    unpack(gmsg, put)
    for m in range(2):
        left = kept[pl.ds(m * N, N), :]
        right = kept[pl.ds((2 + m) * N, N), :]
        grad = prod[pl.ds(m * N, N), :]
        if incoming:
            grad_left, grad_right = dot(right, grad, 1, 1), dot(left, grad, 1, 0)
        else:
            grad_left, grad_right = dot(grad, right, 1, 0), dot(grad, left, 0, 0)
        sides[pl.ds(m * N, N), :] = grad_left.astype(BF)
        sides[pl.ds((2 + m) * N, N), :] = grad_right.astype(BF)

    def piece(q, big):
        t, m, r = q // 8, (q // 4) % 2, q % 4
        return sides[pl.ds((2 * t + m) * N + 64 * r + 16 * big, 16), :]

    pack(msg, piece)


def project_grad(cells, r, nb, w):
    left, left_s, right, right_s = gated(nb, w)
    grad_left = cells[pl.ds(r * C, C), :].astype(F32) * left_s
    grad_right = cells[pl.ds((ROWS + r) * C, C), :].astype(F32) * right_s
    return jnp.concatenate(
        [
            grad_left.astype(BF),
            (grad_left * left * (1.0 - left_s)).astype(BF),
            grad_right.astype(BF),
            (grad_right * right * (1.0 - right_s)).astype(BF),
        ],
        0,
    )


def input_grad(grad_u, normed, inv, grad_proj, grad_gate, w):
    grad = dot(w[:, : 4 * C], grad_proj, 1, 0) + dot(w[:, 4 * C :], grad_gate, 1, 0)
    return grad_u + norm_back(normed, inv, grad)


def back_kernel(
    gmsg, z1, gg2, cot_t, w2, u_t, prod1, w1, v1, msg, sums, grad_u, mix, cells, grad_prod
):
    unpack_pair(gmsg, cells)
    w_in, w, v = w2[...], w1[...], v1[...]
    total = 0.0
    for r in range(ROWS):
        normed, inv = norm(row(z1, r))
        nb = normed.astype(BF)
        grad_proj = project_grad(cells, r, nb, w_in)
        total = total + dot(grad_proj, nb, 1, 1)
        grad = input_grad(row(cot_t, r).astype(F32), normed, inv, grad_proj, row(gg2, r), w_in)
        grad_u[pl.ds(r * C, C), :] = grad
        gate = gate_of(norm(row(u_t, r).astype(F32))[0].astype(BF), w)
        grad_mix = (grad * gate).astype(BF)
        mix[pl.ds(r * C, C), :] = grad_mix
        normed, inv = norm(row(prod1, r).astype(F32))
        grad_prod[pl.ds(r * C, C), :] = norm_back(normed, inv, dot(v, grad_mix, 1, 0)).astype(BF)
    pack_one(msg, grad_prod)
    sums[...] = total.astype(BF)


def last_kernel(gmsg, u_t, w1, own, other, msg, proj, cells):
    unpack_pair(gmsg, cells)
    w = w1[...]
    total = 0.0
    for r in range(ROWS):
        nb = norm(row(u_t, r).astype(F32))[0].astype(BF)
        grad_proj = project_grad(cells, r, nb, w)
        proj[pl.ds(4 * r * C, 4 * C), :] = grad_proj
        total = total + dot(grad_proj, nb, 1, 1)
    early = own[...].astype(F32) + other[...].astype(F32)
    both = jnp.concatenate([total.reshape(64, 1, 8, C), early.reshape(64, 1, 8, C)], axis=1)
    msg[...] = both.reshape(8 * C, C).astype(BF)


def pair_kernel(u_t, proj, gg1, grad_u, w1, out):
    order = column_order()
    w = w1[...]
    for r in range(ROWS):
        normed, inv = norm(row(u_t, r).astype(F32))
        grad = input_grad(
            row(grad_u, r), normed, inv, proj[pl.ds(4 * r * C, 4 * C), :], row(gg1, r), w
        )
        out[r] = dot(order, grad.astype(BF), 0, 1).astype(BF)


def finish_kernel(sums, oi, oo, ii, io):
    groups = sums[...].astype(F32).reshape(64, 3, 8, C)
    for g, w in ((0, oi), (1, ii)):
        part = groups[:, g].reshape(4 * C, C)
        for b in range(4):
            w[:, pl.ds(b * C, C)] = part[b * C : (b + 1) * C].T
    part = groups[:, 2].reshape(4 * C, C)
    for g, w, v in ((0, ii, io), (2, oi, oo)):
        w[:, pl.ds(4 * C, C)] = part[g * C : (g + 1) * C]
        v[...] = part[(g + 1) * C : (g + 2) * C]


def call(kernel, outs, scratch, *args, name, flops=2e8, ordered=0):
    shapes = [jax.ShapeDtypeStruct(s, d) for s, d in outs]
    specs = [pl.BlockSpec(memory_space=pltpu.VMEM)] * (len(args) - ordered)
    specs += [pl.BlockSpec(memory_space=pl.ANY)] * ordered
    moved = sum(a.size * a.dtype.itemsize for a in args)
    moved += sum(s.size * s.dtype.itemsize for s in shapes)
    return pl.pallas_call(
        kernel,
        out_shape=shapes,
        in_specs=specs,
        scratch_shapes=[pltpu.VMEM(s, d) for s, d in scratch],
        compiler_params=pltpu.CompilerParams(vmem_limit_bytes=VMEM_LIMIT),
        cost_estimate=pl.CostEstimate(
            flops=int(flops), bytes_accessed=int(moved), transcendentals=0
        ),
        name=name,
    )(*args)


def exchange(msg):
    shape = msg.shape
    out = lax.all_to_all(msg.reshape(64, 16, shape[1]), "dap", 0, 0, tiled=True)
    return out.reshape(shape)


def pass_on(array):
    reps, devices = lax.axis_size("rep"), lax.axis_size("dap")
    pairs = [
        (rep * devices + d, rep * devices + (d ^ 4))
        for rep in range(0, reps, 2)
        for d in range(devices)
    ]
    return lax.ppermute(array, ("rep", "dap"), pairs)


ONE = (ROWS * C, N)
TWO = (2 * ROWS * C, N)
ONE_MSG = (64 * 16, 128)
TWO_MSG = (64 * 16, 256)
PROJ = (4 * ROWS * C, N)


def product(msg, incoming):
    def kernel(*refs):
        product_kernel(incoming, *refs)

    return call(
        kernel, [((4 * N, N), BF), (ONE_MSG, BF)], [((2 * N, N), BF)], msg, name="product"
    )


def grads(gmsg, kept, incoming):
    def kernel(*refs):
        grads_kernel(incoming, *refs)

    return call(
        kernel, [(TWO_MSG, BF)], [((2 * N, N), BF), ((4 * N, N), BF)], gmsg, kept, name="grads"
    )[0]


def local(pair_act, cotangent, w1, v1, w2, v2):
    lr1, u_t = call(
        first_kernel, [(TWO_MSG, BF), (ONE, BF)], [(TWO, BF)], pair_act[0], w1, pass_on(v1), name="first", ordered=1
    )
    kept1, pmsg1 = product(exchange(lr1), False)
    lr2, z1, prod1 = call(
        middle_kernel,
        [(TWO_MSG, BF), (ONE, F32), (ONE, BF)],
        [(TWO, BF)],
        exchange(pmsg1), u_t, w1, v1, w2,
        name="middle",
    )
    cot_t, mix2, grad_on2 = call(
        cotangent_kernel,
        [(ONE, BF), (ONE, BF), (ONE, F32)],
        [],
        cotangent[0], z1, w2, v2,
        name="cotangent",
    )
    kept2, pmsg2 = product(exchange(lr2), True)
    gmsg2, prod2 = call(
        turn_kernel, [(ONE_MSG, BF), (ONE, BF)], [(ONE, BF)], exchange(pmsg2), grad_on2, name="turn"
    )
    gg2, gv2 = call(
        late_kernel,
        [(ONE, BF), ((2 * C, C), BF)],
        [],
        cot_t, mix2, prod2, z1, w2, v2,
        name="late_incoming",
    )
    gsides2 = grads(exchange(gmsg2), kept2, True)
    gmsg1, sums2, grad_u1, mix1 = call(
        back_kernel,
        [(ONE_MSG, BF), ((4 * C, C), BF), (ONE, F32), (ONE, BF)],
        [(TWO, BF), (ONE, BF)],
        exchange(gsides2), z1, gg2, cot_t, w2, u_t, prod1, w1, v1,
        name="back",
    )
    gg1, gv1 = call(
        late_kernel,
        [(ONE, BF), ((2 * C, C), BF)],
        [],
        grad_u1, mix1, prod1, u_t, w1, v1,
        name="late_outgoing",
    )
    gates = jnp.concatenate([gv2, gv1], 0)
    first_core = lax.axis_index("rep") % 2 == 0
    own = jnp.where(first_core, sums2, gates)
    swaps = [(rep, rep ^ 1) for rep in range(lax.axis_size("rep"))]
    other = lax.ppermute(jnp.where(first_core, gates, sums2), "rep", swaps)
    gsides1 = grads(exchange(gmsg1), kept1, False)
    wmsg, proj1 = call(
        last_kernel,
        [((8 * C, C), BF), (PROJ, BF)],
        [(TWO, BF)],
        exchange(gsides1), u_t, w1, own, other,
        name="last",
    )
    pair_grad = call(
        pair_kernel, [((ROWS, N, C), BF)], [], u_t, proj1, gg1, grad_u1, w1, name="pair"
    )[0]

    scale = 1.0 / math.sqrt(lax.axis_size("rep") * pair_act.shape[0] * N * N)
    parts = lax.all_to_all(wmsg.reshape(64, 16, C), "dap", 0, 0, tiled=True)
    part = jnp.sum(parts.astype(F32), axis=0)
    reps = lax.axis_size("rep")
    across = lax.all_to_all(jnp.broadcast_to(part, (reps, 16, C)), "rep", 0, 0, tiled=True)
    across = across.reshape(reps // 2, 2, 2, 8, C)
    whole = jnp.concatenate(
        [jnp.sum(across[:, :, 0], axis=(0, 1)), jnp.sum(across[:, :, 1], axis=0).reshape(16, C)], 0
    )
    whole = (whole * scale).astype(BF)
    everywhere = lax.all_to_all(jnp.broadcast_to(whole, (64, 24, C)), "dap", 0, 0, tiled=True)
    oi, oo, ii, io = call(
        finish_kernel,
        [((C, 5 * C), F32), ((C, C), F32), ((C, 5 * C), F32), ((C, C), F32)],
        [],
        everywhere.reshape(12 * C, C),
        name="finish",
    )
    return pair_grad[None], oi, oo, ii, io


def solution(mesh):
    return jax.shard_map(
        local,
        mesh=mesh,
        in_specs=(P("rep", "dap", None, None), P("rep", "dap", None, None), P(), P(), P(), P()),
        out_specs=(P("rep", "dap", None, None), P(), P(), P(), P()),
        check_vma=False,
    )
```

```python
import math

import jax
import jax.numpy as jnp
from jax import lax
from jax.experimental import pallas as pl
from jax.experimental.pallas import tpu as pltpu
from jax.sharding import PartitionSpec as P

EPS = 1e-05
ROWS = 4
N = 256
C = 128
BF = jnp.bfloat16
F32 = jnp.float32
VMEM_LIMIT = 48 * 1024 * 1024


def dot(a, b, ca, cb):
    return lax.dot_general(a, b, (((ca,), (cb,)), ((), ())), preferred_element_type=F32)


def swap():
    row = lax.broadcasted_iota(jnp.int32, (256, 256), 0)
    col = lax.broadcasted_iota(jnp.int32, (256, 256), 1)
    hit = ((row & 15) == (col >> 4)) & ((row >> 4) == (col & 15))
    return jnp.where(hit, 1.0, 0.0).astype(BF)


def column_order():
    row = lax.broadcasted_iota(jnp.int32, (N, N), 0)
    col = lax.broadcasted_iota(jnp.int32, (N, N), 1)
    return jnp.where(col == 4 * (row & 63) + (row >> 6), 1.0, 0.0).astype(BF)


def norm(x):
    centred = x - jnp.mean(x, axis=0, keepdims=True)
    inv = lax.rsqrt(jnp.mean(centred * centred, axis=0, keepdims=True) + EPS)
    return centred * inv, inv


def norm_back(normed, inv, grad):
    first = jnp.mean(grad, axis=0, keepdims=True)
    second = jnp.mean(grad * normed, axis=0, keepdims=True)
    return inv * (grad - first - normed * second)


def pack(msg, piece):
    s = swap()
    for big in range(4):
        x = jnp.concatenate([piece(q, big) for q in range(16)], axis=0)
        msg[pl.ds(256 * big, 256), :] = dot(s, x, 1, 0).astype(BF)


def unpack(msg, put):
    s = swap()
    for big in range(4):
        y = dot(s, msg[pl.ds(256 * big, 256), :], 1, 0).astype(BF)
        for q in range(16):
            put(q, big, y[16 * q : 16 * q + 16, :])


def pack_pair(msg, cells):
    def piece(q, big):
        t, m, r = q // 8, (q // 4) % 2, q % 4
        return cells[pl.ds((t * ROWS + r) * C + m * 64 + 16 * big, 16), :]

    pack(msg, piece)


def unpack_pair(msg, cells):
    def put(q, big, rows):
        t, m, r = q // 8, (q // 4) % 2, q % 4
        cells[pl.ds((t * ROWS + r) * C + m * 64 + 16 * big, 16), :] = rows

    unpack(msg, put)


def pack_one(msg, cells):
    def piece(q, big):
        h, m, r = q // 8, (q // 4) % 2, q % 4
        return cells[pl.ds(r * C + m * 64 + 16 * big, 16), pl.ds(128 * h, 128)]

    pack(msg, piece)


def unpack_one(msg, cells):
    def put(q, big, rows):
        h, m, r = q // 8, (q // 4) % 2, q % 4
        cells[pl.ds(r * C + m * 64 + 16 * big, 16), pl.ds(128 * h, 128)] = rows

    unpack(msg, put)


def row(ref, r):
    return ref[pl.ds(r * C, C), :]


def gated(nb, w):
    pre = dot(w[:, : 4 * C], nb, 0, 0)
    return pre[:C], jax.nn.sigmoid(pre[C : 2 * C]), pre[2 * C : 3 * C], jax.nn.sigmoid(pre[3 * C :])


def gate_of(nb, w):
    return jax.nn.sigmoid(dot(w[:, 4 * C :], nb, 0, 0))


def operands(state, w, r, cells):
    normed, _ = norm(state)
    left, left_s, right, right_s = gated(normed.astype(BF), w)
    cells[pl.ds(r * C, C), :] = (left_s * left).astype(BF)
    cells[pl.ds((ROWS + r) * C, C), :] = (right_s * right).astype(BF)


def first_kernel(u, w1, turn, msg, u_t, cells):
    order = column_order()
    w = w1[...]
    for r in range(ROWS):
        state = dot(u[r], order, 0, 1)
        u_t[pl.ds(r * C, C), :] = state.astype(BF)
        operands(state, w, r, cells)
    pack_pair(msg, cells)


def product_kernel(incoming, msg, kept, out, prod):
    def put(q, big, rows):
        t, m, r = q // 8, (q // 4) % 2, q % 4
        kept[pl.ds((2 * t + m) * N + 64 * r + 16 * big, 16), :] = rows

    unpack(msg, put)
    over = 0 if incoming else 1
    for m in range(2):
        left = kept[pl.ds(m * N, N), :]
        right = kept[pl.ds((2 + m) * N, N), :]
        prod[pl.ds(m * N, N), :] = dot(left, right, over, over).astype(BF)

    def piece(q, big):
        h, m, r = q // 8, (q // 4) % 2, q % 4
        return prod[pl.ds(m * N + 64 * r + 16 * big, 16), pl.ds(128 * h, 128)]

    pack(out, piece)


def middle_kernel(pmsg, u_t, w1, v1, w2, msg, z1, prod, cells):
    unpack_one(pmsg, prod)
    w, v, w_next = w1[...], v1[...], w2[...]
    for r in range(ROWS):
        state = row(u_t, r).astype(F32)
        gate = gate_of(norm(state)[0].astype(BF), w)
        out_bf = norm(row(prod, r).astype(F32))[0].astype(BF)
        state = state + gate * dot(v, out_bf, 0, 0)
        z1[pl.ds(r * C, C), :] = state
        operands(state, w_next, r, cells)
    pack_pair(msg, cells)


def cotangent_kernel(cot, z1, w2, v2, cot_t, mix, grad_on):
    order = column_order()
    w, v = w2[...], v2[...]
    for r in range(ROWS):
        grad_u = dot(cot[r], order, 0, 1)
        cot_t[pl.ds(r * C, C), :] = grad_u.astype(BF)
        gate = gate_of(norm(row(z1, r))[0].astype(BF), w)
        grad_mix = (grad_u * gate).astype(BF)
        mix[pl.ds(r * C, C), :] = grad_mix
        grad_on[pl.ds(r * C, C), :] = dot(v, grad_mix, 1, 0)


def turn_kernel(pmsg, grad_on, msg, prod, cells):
    unpack_one(pmsg, prod)
    for r in range(ROWS):
        normed, inv = norm(row(prod, r).astype(F32))
        cells[pl.ds(r * C, C), :] = norm_back(normed, inv, row(grad_on, r)).astype(BF)
    pack_one(msg, cells)


def gate_grads(grad_u, mix, prod, state, w, v):
    nb = norm(state)[0].astype(BF)
    gate = gate_of(nb, w)
    out_bf = norm(prod.astype(F32))[0].astype(BF)
    mixed = dot(v, out_bf, 0, 0)
    grad_gate = (grad_u * mixed * gate * (1.0 - gate)).astype(BF)
    return grad_gate, dot(out_bf, mix, 1, 1), dot(nb, grad_gate, 1, 1)


def late_kernel(grad_u, mix, prod, state, w_ref, v_ref, grad_gate, sums):
    w, v = w_ref[...], v_ref[...]
    grad_v = grad_w = 0.0
    for r in range(ROWS):
        gg, gv, gw = gate_grads(
            row(grad_u, r).astype(F32), row(mix, r), row(prod, r), row(state, r).astype(F32), w, v
        )
        grad_gate[pl.ds(r * C, C), :] = gg
        grad_v = grad_v + gv
        grad_w = grad_w + gw
    sums[pl.ds(0, C), :] = grad_w.astype(BF)
    sums[pl.ds(C, C), :] = grad_v.astype(BF)


def grads_kernel(incoming, gmsg, kept, turn, msg, prod, sides):
    def put(q, big, rows):
        h, m, r = q // 8, (q // 4) % 2, q % 4
        prod[pl.ds(m * N + 64 * r + 16 * big, 16), pl.ds(128 * h, 128)] = rows

    unpack(gmsg, put)
    for m in range(2):
        left = kept[pl.ds(m * N, N), :]
        right = kept[pl.ds((2 + m) * N, N), :]
        grad = prod[pl.ds(m * N, N), :]
        if incoming:
            grad_left, grad_right = dot(right, grad, 1, 1), dot(left, grad, 1, 0)
        else:
            grad_left, grad_right = dot(grad, right, 1, 0), dot(grad, left, 0, 0)
        sides[pl.ds(m * N, N), :] = grad_left.astype(BF)
        sides[pl.ds((2 + m) * N, N), :] = grad_right.astype(BF)

    def piece(q, big):
        t, m, r = q // 8, (q // 4) % 2, q % 4
        return sides[pl.ds((2 * t + m) * N + 64 * r + 16 * big, 16), :]

    pack(msg, piece)


def project_grad(cells, r, nb, w):
    left, left_s, right, right_s = gated(nb, w)
    grad_left = cells[pl.ds(r * C, C), :].astype(F32) * left_s
    grad_right = cells[pl.ds((ROWS + r) * C, C), :].astype(F32) * right_s
    return jnp.concatenate(
        [
            grad_left.astype(BF),
            (grad_left * left * (1.0 - left_s)).astype(BF),
            grad_right.astype(BF),
            (grad_right * right * (1.0 - right_s)).astype(BF),
        ],
        0,
    )


def input_grad(grad_u, normed, inv, grad_proj, grad_gate, w):
    grad = dot(w[:, : 4 * C], grad_proj, 1, 0) + dot(w[:, 4 * C :], grad_gate, 1, 0)
    return grad_u + norm_back(normed, inv, grad)


def back_kernel(
    gmsg, z1, gg2, cot_t, w2, u_t, prod1, w1, v1, msg, sums, grad_u, mix, cells, grad_prod
):
    unpack_pair(gmsg, cells)
    w_in, w, v = w2[...], w1[...], v1[...]
    total = 0.0
    for r in range(ROWS):
        normed, inv = norm(row(z1, r))
        nb = normed.astype(BF)
        grad_proj = project_grad(cells, r, nb, w_in)
        total = total + dot(grad_proj, nb, 1, 1)
        grad = input_grad(row(cot_t, r).astype(F32), normed, inv, grad_proj, row(gg2, r), w_in)
        grad_u[pl.ds(r * C, C), :] = grad
        gate = gate_of(norm(row(u_t, r).astype(F32))[0].astype(BF), w)
        grad_mix = (grad * gate).astype(BF)
        mix[pl.ds(r * C, C), :] = grad_mix
        normed, inv = norm(row(prod1, r).astype(F32))
        grad_prod[pl.ds(r * C, C), :] = norm_back(normed, inv, dot(v, grad_mix, 1, 0)).astype(BF)
    pack_one(msg, grad_prod)
    sums[...] = total.astype(BF)


def last_kernel(gmsg, u_t, w1, own, other, msg, proj, cells):
    unpack_pair(gmsg, cells)
    w = w1[...]
    total = 0.0
    for r in range(ROWS):
        nb = norm(row(u_t, r).astype(F32))[0].astype(BF)
        grad_proj = project_grad(cells, r, nb, w)
        proj[pl.ds(4 * r * C, 4 * C), :] = grad_proj
        total = total + dot(grad_proj, nb, 1, 1)
    early = own[...].astype(F32) + other[...].astype(F32)
    both = jnp.concatenate([total.reshape(64, 1, 8, C), early.reshape(64, 1, 8, C)], axis=1)
    msg[...] = both.reshape(8 * C, C).astype(BF)


def pair_kernel(u_t, proj, gg1, grad_u, w1, out):
    order = column_order()
    w = w1[...]
    for r in range(ROWS):
        normed, inv = norm(row(u_t, r).astype(F32))
        grad = input_grad(
            row(grad_u, r), normed, inv, proj[pl.ds(4 * r * C, 4 * C), :], row(gg1, r), w
        )
        out[r] = dot(order, grad.astype(BF), 0, 1).astype(BF)


def finish_kernel(sums, oi, oo, ii, io):
    groups = sums[...].astype(F32).reshape(64, 3, 8, C)
    for g, w in ((0, oi), (1, ii)):
        part = groups[:, g].reshape(4 * C, C)
        for b in range(4):
            w[:, pl.ds(b * C, C)] = part[b * C : (b + 1) * C].T
    part = groups[:, 2].reshape(4 * C, C)
    for g, w, v in ((0, ii, io), (2, oi, oo)):
        w[:, pl.ds(4 * C, C)] = part[g * C : (g + 1) * C]
        v[...] = part[(g + 1) * C : (g + 2) * C]


def call(kernel, outs, scratch, *args, name, flops=2e8, ordered=0):
    shapes = [jax.ShapeDtypeStruct(s, d) for s, d in outs]
    specs = [pl.BlockSpec(memory_space=pltpu.VMEM)] * (len(args) - ordered)
    specs += [pl.BlockSpec(memory_space=pl.ANY)] * ordered
    moved = sum(a.size * a.dtype.itemsize for a in args)
    moved += sum(s.size * s.dtype.itemsize for s in shapes)
    return pl.pallas_call(
        kernel,
        out_shape=shapes,
        in_specs=specs,
        scratch_shapes=[pltpu.VMEM(s, d) for s, d in scratch],
        compiler_params=pltpu.CompilerParams(vmem_limit_bytes=VMEM_LIMIT),
        cost_estimate=pl.CostEstimate(
            flops=int(flops), bytes_accessed=int(moved), transcendentals=0
        ),
        name=name,
    )(*args)


def exchange(msg):
    shape = msg.shape
    out = lax.all_to_all(msg.reshape(64, 16, shape[1]), "dap", 0, 0, tiled=True)
    return out.reshape(shape)


def pass_on(array, core):
    reps, devices = lax.axis_size("rep"), lax.axis_size("dap")
    pairs = [
        (rep * devices + d, rep * devices + (d ^ 4))
        for rep in range(core, reps, 2)
        for d in range(devices)
    ]
    return lax.ppermute(array, ("rep", "dap"), pairs)


ONE = (ROWS * C, N)
TWO = (2 * ROWS * C, N)
ONE_MSG = (64 * 16, 128)
TWO_MSG = (64 * 16, 256)
PROJ = (4 * ROWS * C, N)


def product(msg, incoming):
    def kernel(*refs):
        product_kernel(incoming, *refs)

    return call(
        kernel, [((4 * N, N), BF), (ONE_MSG, BF)], [((2 * N, N), BF)], msg, name="product"
    )


def grads(gmsg, kept, turn, incoming):
    def kernel(*refs):
        grads_kernel(incoming, *refs)

    return call(
        kernel, [(TWO_MSG, BF)], [((2 * N, N), BF), ((4 * N, N), BF)], gmsg, kept, turn, name="grads", ordered=1
    )[0]


def local(pair_act, cotangent, w1, v1, w2, v2):
    lr1, u_t = call(
        first_kernel, [(TWO_MSG, BF), (ONE, BF)], [(TWO, BF)], pair_act[0], w1, pass_on(v1, 0), name="first", ordered=1
    )
    kept1, pmsg1 = product(exchange(lr1), False)
    lr2, z1, prod1 = call(
        middle_kernel,
        [(TWO_MSG, BF), (ONE, F32), (ONE, BF)],
        [(TWO, BF)],
        exchange(pmsg1), u_t, w1, v1, w2,
        name="middle",
    )
    cot_t, mix2, grad_on2 = call(
        cotangent_kernel,
        [(ONE, BF), (ONE, BF), (ONE, F32)],
        [],
        cotangent[0], z1, w2, v2,
        name="cotangent",
    )
    kept2, pmsg2 = product(exchange(lr2), True)
    gmsg2, prod2 = call(
        turn_kernel, [(ONE_MSG, BF), (ONE, BF)], [(ONE, BF)], exchange(pmsg2), grad_on2, name="turn"
    )
    gg2, gv2 = call(
        late_kernel,
        [(ONE, BF), ((2 * C, C), BF)],
        [],
        cot_t, mix2, prod2, z1, w2, v2,
        name="late_incoming",
    )
    gsides2 = grads(exchange(gmsg2), kept2, v2, True)
    gmsg1, sums2, grad_u1, mix1 = call(
        back_kernel,
        [(ONE_MSG, BF), ((4 * C, C), BF), (ONE, F32), (ONE, BF)],
        [(TWO, BF), (ONE, BF)],
        exchange(gsides2), z1, gg2, cot_t, w2, u_t, prod1, w1, v1,
        name="back",
    )
    gg1, gv1 = call(
        late_kernel,
        [(ONE, BF), ((2 * C, C), BF)],
        [],
        grad_u1, mix1, prod1, u_t, w1, v1,
        name="late_outgoing",
    )
    gates = jnp.concatenate([gv2, gv1], 0)
    first_core = lax.axis_index("rep") % 2 == 0
    own = jnp.where(first_core, sums2, gates)
    swaps = [(rep, rep ^ 1) for rep in range(lax.axis_size("rep"))]
    other = lax.ppermute(jnp.where(first_core, gates, sums2), "rep", swaps)
    grad_ch = exchange(gmsg1)
    gsides1 = grads(grad_ch, kept1, pass_on(grad_ch, 1), False)
    wmsg, proj1 = call(
        last_kernel,
        [((8 * C, C), BF), (PROJ, BF)],
        [(TWO, BF)],
        exchange(gsides1), u_t, w1, own, other,
        name="last",
    )
    pair_grad = call(
        pair_kernel, [((ROWS, N, C), BF)], [], u_t, proj1, gg1, grad_u1, w1, name="pair"
    )[0]

    scale = 1.0 / math.sqrt(lax.axis_size("rep") * pair_act.shape[0] * N * N)
    parts = lax.all_to_all(wmsg.reshape(64, 16, C), "dap", 0, 0, tiled=True)
    part = jnp.sum(parts.astype(F32), axis=0)
    reps = lax.axis_size("rep")
    across = lax.all_to_all(jnp.broadcast_to(part, (reps, 16, C)), "rep", 0, 0, tiled=True)
    across = across.reshape(reps // 2, 2, 2, 8, C)
    whole = jnp.concatenate(
        [jnp.sum(across[:, :, 0], axis=(0, 1)), jnp.sum(across[:, :, 1], axis=0).reshape(16, C)], 0
    )
    whole = (whole * scale).astype(BF)
    everywhere = lax.all_to_all(jnp.broadcast_to(whole, (64, 24, C)), "dap", 0, 0, tiled=True)
    oi, oo, ii, io = call(
        finish_kernel,
        [((C, 5 * C), F32), ((C, C), F32), ((C, 5 * C), F32), ((C, C), F32)],
        [],
        everywhere.reshape(12 * C, C),
        name="finish",
    )
    return pair_grad[None], oi, oo, ii, io


def solution(mesh):
    return jax.shard_map(
        local,
        mesh=mesh,
        in_specs=(P("rep", "dap", None, None), P("rep", "dap", None, None), P(), P(), P(), P()),
        out_specs=(P("rep", "dap", None, None), P(), P(), P(), P()),
        check_vma=False,
    )
```
